256 devices in a mesh: chan: 8 (over z_hi, x), depth: 32 (over z_lo, y, core).
Axes of the slice: x: 4, y: 4, z: 8 (z_hi: 2, z_lo: 4; z = z_hi * 4 + z_lo), core: 2. Of those that a mesh axis runs over, the one named last changes fastest.
Arguments:
- volume: float32 [256, 32, 16, 128], P('chan', 'depth'), may hold values from -6 to 6
- kernel: float32 [3, 3, 3, 256, 256], P(None, None, None, 'chan'), may hold values from -0.078125 to 0.078125
Outputs:
- response: float32 [256, 32, 16, 128], P('chan', 'depth')
The draws below stay inside these ranges and needn't reach their ends.
All inputs are finite; a program needn't handle non-finite values.
Results may differ from the reference program's by a relative error of at most 0.0001.
Values sent between devices are 32-bit elements; how exact they have to be, the bound alone decides.
No kernel may reach another device: no remote copies, remote signals or barrier semaphores. Data moves between devices by JAX's collectives and lax.ppermute only.
A program may use at most 128 MiB of HBM per device.

```python
import jax
import jax.numpy as jnp
from jax import lax

C_IN = 256
C_OUT = 256
H = 16
W = 128
DEPTH = 32


def level_of(rng, extent, shards, smallest, largest):
    loudness, own = 1.0, jax.random.fold_in(rng, 6)
    for position, blocks in shards:
        steps = jnp.exp(jax.random.uniform(jax.random.fold_in(own, position), (blocks,), jnp.float32, smallest / len(shards), largest / len(shards)))
        loudness = loudness * jnp.repeat(steps, extent[position] // blocks).reshape([-1 if axis == position else 1 for axis in range(len(extent))])
    return loudness


def centred(key, extent, scale, most, pieces=(), kind=jnp.bfloat16):
    values = scale * jax.random.normal(key, extent, jnp.float32)
    if pieces:
        values = values * level_of(key, extent, pieces, -0.22, 0.18)
    return jnp.clip(values, -most, most).astype(kind)


def setup_inputs(seed: int = 0) -> dict:
    splits = jax.random.split(jax.random.key(seed), 3)
    return {
        "volume": centred(splits[0], (C_IN, DEPTH, H, W), 1.0, 6.0, ((0, 8), (1, 32)), jnp.float32),
        "kernel": centred(splits[1], (3, 3, 3, C_OUT, C_IN), (27 * C_IN) ** -0.5, 0.078125, ((3, 8),), jnp.float32),
    }


def spread(volume, taps):
    channels, planes, height, across = volume.shape
    filters = taps.shape[2]
    framed = jnp.pad(volume, ((0, 0), (0, 0), (1, 1), (0, 0)))
    running = jnp.zeros((filters, planes, height, across), jnp.float32)
    for row_tap in range(3):
        column_slab = framed[:, :, row_tap:row_tap + height, :].reshape(channels, planes * height * across)
        products = jnp.dot(taps[row_tap].reshape(3 * filters, channels), column_slab,
                           precision=lax.Precision.HIGHEST, preferred_element_type=jnp.float32)
        products = products.reshape(3, filters, planes, height, across)
        lower_tap = jnp.pad(products[0], ((0, 0), (0, 0), (0, 0), (1, 0)))[..., :across]
        upper_tap = jnp.pad(products[2], ((0, 0), (0, 0), (0, 0), (0, 1)))[..., 1:]
        running = running + products[1] + lower_tap + upper_tap
    return running


def reference(volume, kernel):
    planes = volume.shape[1]
    padded = jnp.pad(volume, ((0, 0), (1, 1), (0, 0), (0, 0)))
    response = spread(padded[:, 0:planes], kernel[0])
    for depth_tap in range(1, 3):
        response = response + spread(padded[:, depth_tap:depth_tap + planes], kernel[depth_tap])
    return response
```

```python
import jax
import jax.numpy as jnp
from jax import lax
from jax.experimental import pallas as pl
from jax.experimental.pallas import tpu as pltpu
from jax.sharding import PartitionSpec as P

X = 4
F32, BF16 = jnp.float32, jnp.bfloat16


def split(values):
    high = values.astype(BF16)
    return high, (values - high.astype(F32)).astype(BF16)


def taps_kernel(kernel_ref, near_ref, far_ref):
    me = lax.axis_index("chan")
    core = lax.rem(lax.axis_index("depth"), 2)
    z, x = me // X, lax.rem(me, X)
    filters = kernel_ref.shape[3]
    half = kernel_ref.shape[4] // 2
    turn = lax.rem(half - (half // X) * x, half)
    for out_ref, row in ((near_ref, z), (far_ref, 1 - z)):
        columns = pl.ds(pl.multiple_of(row * half, half), half)
        for a, plane in enumerate((2 - 2 * core, 2 * core, 1)):
            for b in range(3):
                rows = pl.ds((a * 3 + b) * filters, filters)
                for e in range(3):
                    high, low = split(
                        pltpu.roll(kernel_ref[plane, b, e, :, columns], turn, 1)
                    )
                    out_ref[rows, pl.ds(e * half, half)] = high
                    out_ref[rows, pl.ds((3 + e) * half, half)] = high
                    out_ref[rows, pl.ds((6 + e) * half, half)] = low


def accumulate(shards, taps_ref, cells, total):
    across = shards[0].shape[1]
    height = cells.shape[1] // across
    channels = shards[0].shape[0] // height
    half = channels * len(shards)
    filters = total.shape[0] // 3
    lane = lax.broadcasted_iota(jnp.int32, (channels, across), 1)
    total[...] = jnp.zeros_like(total)
    step = 2
    for start in range(0, height, step):
        for h in range(start, start + step):
            for k, ref in enumerate(shards):
                middle = ref[pl.ds(h, channels, stride=height), :]
                left = jnp.where(lane == 0, 0.0, pltpu.roll(middle, 1, 1))
                right = jnp.where(lane == across - 1, 0.0, pltpu.roll(middle, across - 1, 1))
                for e, values in enumerate((left, middle, right)):
                    high, low = split(values)
                    row = e * half + k * channels
                    cells[pl.ds(row, channels), pl.ds(h * across, across)] = high
                    cells[pl.ds(3 * half + row, channels), pl.ds(h * across, across)] = low
        wide = pl.ds(start * across, step * across)
        products = jnp.dot(
            taps_ref[:, : 6 * half], cells[:, wide], preferred_element_type=F32
        ) + jnp.dot(
            taps_ref[:, 6 * half :], cells[: 3 * half, wide], preferred_element_type=F32
        )
        for a in range(3):
            for b in range(3):
                row = (a * 3 + b) * filters
                place = pl.ds((start + 2 - b) * across, step * across)
                total[pl.ds(a * filters, filters), place] += products[row : row + filters]


def near_kernel(s0, s1, s2, s3, taps_ref, total, cells):
    accumulate((s0, s1, s2, s3), taps_ref, cells, total)


def far_kernel(s0, s1, s2, s3, taps_ref, near_ref, off_ref, on_ref, mid_ref, cells, total):
    accumulate((s0, s1, s2, s3), taps_ref, cells, total)
    across = s0.shape[1]
    height = cells.shape[1] // across
    filters = total.shape[0] // 3
    for a, out_ref in enumerate((off_ref, on_ref, mid_ref)):
        for h in range(height):
            rows, place = pl.ds(a * filters, filters), pl.ds((h + 1) * across, across)
            out_ref[pl.ds(h, filters, stride=height), :] = total[rows, place] + near_ref[rows, place]


def along_x(step):
    return [(4 * g + i, 4 * g + (i + step) % 4) for g in range(2) for i in range(4)]


def local(volume, kernel):
    filters, channels = kernel.shape[3], kernel.shape[4]
    shard, _, height, across = volume.shape
    half = channels // 2
    cells = shard * height
    limit = pltpu.CompilerParams(vmem_limit_bytes=24 * 1024 * 1024)
    own = volume.reshape(cells, across)
    other = lax.ppermute(own, "chan", [(i, (i + X) % (2 * X)) for i in range(2 * X)])
    near = [own] + [lax.ppermute(own, "chan", along_x(step)) for step in (3, 2, 1)]
    far = [other] + [lax.ppermute(other, "chan", along_x(step)) for step in (3, 2, 1)]
    weights = jax.ShapeDtypeStruct((9 * filters, 9 * half), BF16)
    near_taps, far_taps = pl.pallas_call(
        taps_kernel,
        out_shape=(weights, weights),
        compiler_params=limit,
        cost_estimate=pl.CostEstimate(flops=0, bytes_accessed=4_000_000, transcendentals=0),
        name="taps",
    )(kernel)
    work = pl.CostEstimate(
        flops=2 * 9 * filters * 9 * half * height * across,
        bytes_accessed=4_000_000,
        transcendentals=0,
    )
    total = (3 * filters, (height + 2) * across)
    scratch = pltpu.VMEM((6 * half, height * across), BF16)
    near_total = pl.pallas_call(
        near_kernel,
        out_shape=jax.ShapeDtypeStruct(total, F32),
        scratch_shapes=[scratch],
        compiler_params=limit,
        cost_estimate=work,
        name="near",
    )(*near, near_taps)
    part = jax.ShapeDtypeStruct((filters * height, across), F32)
    off, on, mid = pl.pallas_call(
        far_kernel,
        out_shape=(part, part, part),
        scratch_shapes=[scratch, pltpu.VMEM(total, F32)],
        compiler_params=limit,
        cost_estimate=work,
        name="far",
    )(*far, far_taps, near_total)
    planes = lax.axis_size("depth")
    between = [(i, i + 1) for i in range(1, planes - 1, 2)]
    within = [(i, i + 1) for i in range(0, planes, 2)]
    off = lax.ppermute(off, "depth", between + [(j, i) for i, j in between])
    on = lax.ppermute(on, "depth", within + [(j, i) for i, j in within])
    return (mid + off + on).reshape(filters, 1, height, across)


def solution(mesh):
    return jax.shard_map(
        local,
        mesh=mesh,
        in_specs=(P("chan", "depth", None, None), P(None, None, None, "chan", None)),
        out_specs=P("chan", "depth", None, None),
        check_vma=False,
    )
```

```python
import functools

import jax
import jax.numpy as jnp
from jax import lax
from jax.experimental import pallas as pl
from jax.experimental.pallas import tpu as pltpu
from jax.sharding import PartitionSpec as P

X = 4
ROWS = 2
F32, BF16 = jnp.float32, jnp.bfloat16


def split(values):
    high = values.astype(BF16)
    return high, (values - high.astype(F32)).astype(BF16)


def taps_kernel(kernel_ref, near_ref, far_ref, last_ref):
    me = lax.axis_index("chan")
    core = lax.rem(lax.axis_index("depth"), 2)
    z, x = me // X, lax.rem(me, X)
    filters = kernel_ref.shape[3]
    half = kernel_ref.shape[4] // 2
    shard = half // X
    turn = lax.rem((X - x) * shard, half)
    slot = lax.broadcasted_iota(jnp.int32, (filters, half), 1) // shard
    for out_ref, row in ((near_ref, z), (far_ref, 1 - z)):
        columns = pl.ds(pl.multiple_of(row * half, half), half)
        for a, plane in enumerate((2 - 2 * core, 2 * core, 1)):
            for b in range(3):
                rows = pl.ds((a * 3 + b) * filters, filters)
                blocks = []
                for e in range(3):
                    values = pltpu.roll(kernel_ref[plane, b, e, :, columns], turn, 1)
                    high, low = split(values)
                    out_ref[rows, pl.ds(e * half, half)] = high
                    out_ref[rows, pl.ds((3 + e) * half, half)] = high
                    out_ref[rows, pl.ds((6 + e) * half, half)] = low
                    blocks.append((high.astype(F32), low.astype(F32)))
                if out_ref is far_ref:
                    blocks = [h for h, _ in blocks] * 2 + [l for _, l in blocks]
                    for tile in range(last_ref.shape[1] // half):
                        result = jnp.zeros((filters, half), F32)
                        for k, values in enumerate(blocks[tile * X : tile * X + X]):
                            placed = pltpu.roll(values, (k + X - 2) % X * shard, 1)
                            result = jnp.where(slot == k, placed, result)
                        last_ref[rows, pl.ds(tile * half, half)] = result.astype(BF16)


def pack(ref, cells, h, height, row_sets):
    channels, across = ref.shape[0] // height, ref.shape[1]
    lane = lax.broadcasted_iota(jnp.int32, (channels, across), 1)
    middle = ref[pl.ds(h, channels, stride=height), :]
    left = jnp.where(lane == 0, 0.0, pltpu.roll(middle, 1, 1))
    right = jnp.where(lane == across - 1, 0.0, pltpu.roll(middle, across - 1, 1))
    for values, rows in zip((left, middle, right), row_sets):
        high, low = split(values)
        for row, part in zip(rows, (high, low, high)):
            cells[pl.ds(row, channels), pl.ds(h * across, across)] = part


def accumulate(shards, taps_ref, cells, total):
    across = shards[0].shape[1]
    height = cells.shape[1] // across
    channels = shards[0].shape[0] // height
    half = cells.shape[0] // 6
    for k, ref in enumerate(shards):
        if ref is None:
            for e in range(6):
                rows = pl.ds(e * half + k * channels, channels)
                cells[rows, :] = jnp.zeros((channels, cells.shape[1]), BF16)
    for start in range(0, height, ROWS):
        for h in range(start, start + ROWS):
            for k, ref in enumerate(shards):
                if ref is not None:
                    row = k * channels
                    pack(ref, cells, h, height, [(e * half + row, (3 + e) * half + row) for e in range(3)])
        wide = pl.ds(start * across, ROWS * across)
        products = jnp.dot(
            taps_ref[:, : 6 * half], cells[:, wide], preferred_element_type=F32
        ) + jnp.dot(
            taps_ref[:, 6 * half :], cells[: 3 * half, wide], preferred_element_type=F32
        )
        scatter(products, total, total.shape[0] // 3, start, across)


def scatter(products, total, filters, start, across):
    for a in range(total.shape[0] // filters):
        for b in range(3):
            row = (a * 3 + b) * filters
            place = pl.ds((start + 2 - b) * across, ROWS * across)
            total[pl.ds(a * filters, filters), place] += products[row : row + filters]


def near_kernel(s0, s1, s2, s3, taps_ref, total, cells):
    total[...] = jnp.zeros_like(total)
    accumulate((s0, s1, s2, s3), taps_ref, cells, total)


def far_kernel(s0, s1, s3, taps_ref, near_ref, total, cells):
    total[...] = near_ref[...]
    accumulate((s0, s1, None, s3), taps_ref, cells, total)


def last_kernel(planes, ref, taps_ref, before_ref, *rest):
    *out_refs, cells, total = rest
    across = ref.shape[1]
    height = cells.shape[1] // across
    channels = ref.shape[0] // height
    filters = before_ref.shape[0] // 3
    first = planes[0] * filters
    total[...] = before_ref[pl.ds(first, total.shape[0]), :]
    unused = cells.shape[0] - 9 * channels
    cells[pl.ds(9 * channels, unused), :] = jnp.zeros((unused, cells.shape[1]), BF16)
    for start in range(0, height, ROWS):
        for h in range(start, start + ROWS):
            pack(ref, cells, h, height, [[(3 * t + e) * channels for t in range(3)] for e in range(3)])
        products = jnp.dot(
            taps_ref[pl.ds(3 * first, 3 * total.shape[0]), :],
            cells[:, pl.ds(start * across, ROWS * across)],
            preferred_element_type=F32,
        )
        scatter(products, total, filters, start, across)
    for a, out_ref in enumerate(out_refs):
        for h in range(height):
            out_ref[pl.ds(h, filters, stride=height), :] = total[
                pl.ds(a * filters, filters), pl.ds((h + 1) * across, across)
            ]


def spread(block):
    return [
        lax.ppermute(
            block, "chan", [(g * X + i, g * X + (i - step) % X) for g in range(2) for i in range(X)]
        )
        for step in (1, 3, 2)
    ]


def local(volume, kernel):
    filters, channels = kernel.shape[3], kernel.shape[4]
    shard, _, height, across = volume.shape
    half = channels // 2
    cells = shard * height
    limit = pltpu.CompilerParams(vmem_limit_bytes=24 * 1024 * 1024)
    own = volume.reshape(cells, across)
    other = lax.ppermute(own, "chan", [(i, (i + X) % (2 * X)) for i in range(2 * X)])
    s1, s3, s2 = spread(own)
    t1, t3, t2 = spread(other)
    weights = jax.ShapeDtypeStruct((9 * filters, 9 * half), BF16)
    last_weights = jax.ShapeDtypeStruct((9 * filters, 3 * half), BF16)
    near_taps, far_taps, last_taps = pl.pallas_call(
        taps_kernel,
        out_shape=(weights, weights, last_weights),
        compiler_params=limit,
        cost_estimate=pl.CostEstimate(flops=0, bytes_accessed=4_000_000, transcendentals=0),
        name="taps",
    )(kernel)

    def work(planes, part):
        return pl.CostEstimate(
            flops=int(2 * 3 * planes * filters * 9 * half * part * height * across),
            bytes_accessed=3_000_000,
            transcendentals=0,
        )

    total = jax.ShapeDtypeStruct((3 * filters, (height + 2) * across), F32)
    packed = pltpu.VMEM((6 * half, height * across), BF16)
    before = pl.pallas_call(
        near_kernel,
        out_shape=total,
        scratch_shapes=[packed],
        compiler_params=limit,
        cost_estimate=work(3, 1),
        name="near",
    )(own, s1, s2, s3, near_taps)
    before = pl.pallas_call(
        far_kernel,
        out_shape=total,
        scratch_shapes=[packed],
        compiler_params=limit,
        cost_estimate=work(3, 1),
        name="far",
    )(other, t1, t3, far_taps, before)

    def last(name, *taps):
        part = jax.ShapeDtypeStruct((filters * height, across), F32)
        return pl.pallas_call(
            functools.partial(last_kernel, taps),
            out_shape=[part] * len(taps),
            scratch_shapes=[
                pltpu.VMEM((3 * half, height * across), BF16),
                pltpu.VMEM((len(taps) * filters, total.shape[1]), F32),
            ],
            compiler_params=limit,
            cost_estimate=work(len(taps), 0.25),
            name=name,
        )(t2, last_taps, before)

    (off,) = last("off", 0)
    on, mid = last("rest", 1, 2)
    planes = lax.axis_size("depth")
    between = [(i, i + 1) for i in range(1, planes - 1, 2)]
    within = [(i, i + 1) for i in range(0, planes, 2)]
    off = lax.ppermute(off, "depth", between + [(j, i) for i, j in between])
    on = lax.ppermute(on, "depth", within + [(j, i) for i, j in within])
    return (mid + off + on).reshape(filters, 1, height, across)


def solution(mesh):
    return jax.shard_map(
        local,
        mesh=mesh,
        in_specs=(P("chan", "depth", None, None), P(None, None, None, "chan", None)),
        out_specs=P("chan", "depth", None, None),
        check_vma=False,
    )
```

```python
import functools

import jax
import jax.numpy as jnp
from jax import lax
from jax.experimental import pallas as pl
from jax.experimental.pallas import tpu as pltpu
from jax.sharding import PartitionSpec as P

X = 4
ROWS = 2
F32, BF16 = jnp.float32, jnp.bfloat16


def split(values):
    high = values.astype(BF16)
    return high, (values - high.astype(F32)).astype(BF16)


def taps_kernel(kernel_ref, near_ref, far_ref, last_ref):
    me = lax.axis_index("chan")
    core = lax.rem(lax.axis_index("depth"), 2)
    z, x = me // X, lax.rem(me, X)
    filters = kernel_ref.shape[3]
    half = kernel_ref.shape[4] // 2
    shard = half // X
    turn = lax.rem((X - x) * shard, half)
    slot = lax.broadcasted_iota(jnp.int32, (filters, half), 1) // shard
    for out_ref, row in ((near_ref, z), (far_ref, 1 - z)):
        columns = pl.ds(pl.multiple_of(row * half, half), half)
        for a, plane in enumerate((2 - 2 * core, 2 * core, 1)):
            for b in range(3):
                rows = pl.ds((a * 3 + b) * filters, filters)
                blocks = []
                for e in range(3):
                    values = pltpu.roll(kernel_ref[plane, b, e, :, columns], turn, 1)
                    high, low = split(values)
                    out_ref[rows, pl.ds(e * half, half)] = high
                    out_ref[rows, pl.ds((3 + e) * half, half)] = high
                    out_ref[rows, pl.ds((6 + e) * half, half)] = low
                    blocks.append((high.astype(F32), low.astype(F32)))
                if out_ref is far_ref:
                    blocks = [h for h, _ in blocks] * 2 + [l for _, l in blocks]
                    for tile in range(last_ref.shape[1] // half):
                        result = jnp.zeros((filters, half), F32)
                        for k, values in enumerate(blocks[tile * X : tile * X + X]):
                            placed = pltpu.roll(values, (k + X - 2) % X * shard, 1)
                            result = jnp.where(slot == k, placed, result)
                        last_ref[rows, pl.ds(tile * half, half)] = result.astype(BF16)


def pack(ref, cells, h, height, row_sets):
    channels, across = ref.shape[0] // height, ref.shape[1]
    lane = lax.broadcasted_iota(jnp.int32, (channels, across), 1)
    middle = ref[pl.ds(h, channels, stride=height), :]
    left = jnp.where(lane == 0, 0.0, pltpu.roll(middle, 1, 1))
    right = jnp.where(lane == across - 1, 0.0, pltpu.roll(middle, across - 1, 1))
    for values, rows in zip((left, middle, right), row_sets):
        high, low = split(values)
        for row, part in zip(rows, (high, low, high)):
            cells[pl.ds(row, channels), pl.ds(h * across, across)] = part


def accumulate(shards, taps_ref, cells, total):
    across = shards[0][0].shape[1]
    height = cells.shape[1] // across
    half = cells.shape[0] // 6
    channels = half // X
    for k, refs in enumerate(shards):
        if not refs:
            for e in range(6):
                rows = pl.ds(e * half + k * channels, channels)
                cells[rows, :] = jnp.zeros((channels, cells.shape[1]), BF16)
    for start in range(0, height, ROWS):
        for h in range(start, start + ROWS):
            for k, refs in enumerate(shards):
                for j, ref in enumerate(refs):
                    row = k * channels + j * channels // len(refs)
                    pack(ref, cells, h, height, [(e * half + row, (3 + e) * half + row) for e in range(3)])
        wide = pl.ds(start * across, ROWS * across)
        products = jnp.dot(
            taps_ref[:, : 6 * half], cells[:, wide], preferred_element_type=F32
        ) + jnp.dot(
            taps_ref[:, 6 * half :], cells[: 3 * half, wide], preferred_element_type=F32
        )
        scatter(products, total, total.shape[0] // 3, start, across)


def scatter(products, total, filters, start, across):
    for a in range(total.shape[0] // filters):
        for b in range(3):
            row = (a * 3 + b) * filters
            place = pl.ds((start + 2 - b) * across, ROWS * across)
            total[pl.ds(a * filters, filters), place] += products[row : row + filters]


def near_kernel(s0, s1, s2, s3, taps_ref, total, cells):
    total[...] = jnp.zeros_like(total)
    accumulate(((s0,), (s1,), (s2,), (s3,)), taps_ref, cells, total)


def far_kernel(s0, s1a, s1b, s3a, s3b, taps_ref, near_ref, total, cells):
    total[...] = near_ref[...]
    accumulate(((s0,), (s1a, s1b), (), (s3a, s3b)), taps_ref, cells, total)


def last_kernel(planes, s2a, s2b, taps_ref, before_ref, *rest):
    *out_refs, cells, total = rest
    across = s2a.shape[1]
    height = cells.shape[1] // across
    part = s2a.shape[0] // height
    channels = 2 * part
    filters = before_ref.shape[0] // 3
    first = planes[0] * filters
    total[...] = before_ref[pl.ds(first, total.shape[0]), :]
    unused = cells.shape[0] - 9 * channels
    cells[pl.ds(9 * channels, unused), :] = jnp.zeros((unused, cells.shape[1]), BF16)
    for start in range(0, height, ROWS):
        for h in range(start, start + ROWS):
            for j, ref in enumerate((s2a, s2b)):
                rows = [[(3 * t + e) * channels + j * part for t in range(3)] for e in range(3)]
                pack(ref, cells, h, height, rows)
        products = jnp.dot(
            taps_ref[pl.ds(3 * first, 3 * total.shape[0]), :],
            cells[:, pl.ds(start * across, ROWS * across)],
            preferred_element_type=F32,
        )
        scatter(products, total, filters, start, across)
    for a, out_ref in enumerate(out_refs):
        for h in range(height):
            out_ref[pl.ds(h, filters, stride=height), :] = total[
                pl.ds(a * filters, filters), pl.ds((h + 1) * across, across)
            ]


def from_x(block, step):
    pairs = [(g * X + i, g * X + (i - step) % X) for g in range(2) for i in range(X)]
    return lax.ppermute(block, "chan", pairs)


def divide_kernel(whole_ref, order_ref, low_ref, high_ref):
    low_ref[...] = whole_ref[: low_ref.shape[0]]
    high_ref[...] = whole_ref[low_ref.shape[0] :]


def local(volume, kernel):
    filters, channels = kernel.shape[3], kernel.shape[4]
    shard, _, height, across = volume.shape
    half = channels // 2
    cells = shard * height
    limit = pltpu.CompilerParams(vmem_limit_bytes=24 * 1024 * 1024)
    own = volume.reshape(cells, across)
    other = lax.ppermute(own, "chan", [(i, (i + X) % (2 * X)) for i in range(2 * X)])
    s1, s3, s2 = [from_x(own, step) for step in (1, 3, 2)]
    weights = jax.ShapeDtypeStruct((9 * filters, 9 * half), BF16)
    last_weights = jax.ShapeDtypeStruct((9 * filters, 3 * half), BF16)
    near_taps, far_taps, last_taps = pl.pallas_call(
        taps_kernel,
        out_shape=(weights, weights, last_weights),
        compiler_params=limit,
        cost_estimate=pl.CostEstimate(flops=0, bytes_accessed=4_000_000, transcendentals=0),
        name="taps",
    )(kernel)

    part = jax.ShapeDtypeStruct((cells // 2, across), F32)
    low, high = pl.pallas_call(
        divide_kernel,
        out_shape=(part, part),
        in_specs=[pl.BlockSpec(memory_space=pltpu.VMEM), pl.BlockSpec(memory_space=pl.ANY)],
        compiler_params=limit,
        name="divide",
    )(other, last_taps)
    t3a, t1b = from_x(low, 3), from_x(high, 1)
    t3b, t1a = from_x(high, 3), from_x(low, 1)
    t2a, t2b = from_x(t3a, 3), from_x(t1b, 1)

    def work(planes, part):
        return pl.CostEstimate(
            flops=int(2 * 3 * planes * filters * 9 * half * part * height * across),
            bytes_accessed=3_000_000,
            transcendentals=0,
        )

    total = jax.ShapeDtypeStruct((3 * filters, (height + 2) * across), F32)
    packed = pltpu.VMEM((6 * half, height * across), BF16)
    before = pl.pallas_call(
        near_kernel,
        out_shape=total,
        scratch_shapes=[packed],
        compiler_params=limit,
        cost_estimate=work(3, 1),
        name="near",
    )(own, s1, s2, s3, near_taps)
    before = pl.pallas_call(
        far_kernel,
        out_shape=total,
        scratch_shapes=[packed],
        compiler_params=limit,
        cost_estimate=work(3, 1),
        name="far",
    )(other, t1a, t1b, t3a, t3b, far_taps, before)

    def last(name, *taps):
        part = jax.ShapeDtypeStruct((filters * height, across), F32)
        return pl.pallas_call(
            functools.partial(last_kernel, taps),
            out_shape=[part] * len(taps),
            scratch_shapes=[
                pltpu.VMEM((3 * half, height * across), BF16),
                pltpu.VMEM((len(taps) * filters, total.shape[1]), F32),
            ],
            compiler_params=limit,
            cost_estimate=work(len(taps), 0.25),
            name=name,
        )(t2a, t2b, last_taps, before)

    (off,) = last("off", 0)
    on, mid = last("rest", 1, 2)
    planes = lax.axis_size("depth")
    between = [(i, i + 1) for i in range(1, planes - 1, 2)]
    within = [(i, i + 1) for i in range(0, planes, 2)]
    off = lax.ppermute(off, "depth", between + [(j, i) for i, j in between])
    on = lax.ppermute(on, "depth", within + [(j, i) for i, j in within])
    return (mid + off + on).reshape(filters, 1, height, across)


def solution(mesh):
    return jax.shard_map(
        local,
        mesh=mesh,
        in_specs=(P("chan", "depth", None, None), P(None, None, None, "chan", None)),
        out_specs=P("chan", "depth", None, None),
        check_vma=False,
    )
```

```python
import functools

import jax
import jax.numpy as jnp
from jax import lax
from jax.experimental import pallas as pl
from jax.experimental.pallas import tpu as pltpu
from jax.sharding import PartitionSpec as P

X = 4
ROWS = 2
LIMIT = pltpu.CompilerParams(vmem_limit_bytes=24 * 1024 * 1024)
F32, BF16 = jnp.float32, jnp.bfloat16


def split(values):
    high = values.astype(BF16)
    return high, (values - high.astype(F32)).astype(BF16)


def taps_kernel(kernel_ref, near_ref, far_ref, last_ref):
    me = lax.axis_index("chan")
    core = lax.rem(lax.axis_index("depth"), 2)
    z, x = me // X, lax.rem(me, X)
    filters = kernel_ref.shape[3]
    half = kernel_ref.shape[4] // 2
    shard = half // X
    turn = lax.rem((X - x) * shard, half)
    slot = lax.broadcasted_iota(jnp.int32, (filters, half), 1) // shard
    for out_ref, row in ((near_ref, z), (far_ref, 1 - z)):
        columns = pl.ds(pl.multiple_of(row * half, half), half)
        for a, plane in enumerate((2 - 2 * core, 2 * core, 1)):
            for b in range(3):
                rows = pl.ds((a * 3 + b) * filters, filters)
                blocks = []
                for e in range(3):
                    values = pltpu.roll(kernel_ref[plane, b, e, :, columns], turn, 1)
                    mirrored = pltpu.roll(values, half // 2, 1)
                    high, low = split(jnp.where(slot % 2 * core == 1, mirrored, values))
                    out_ref[rows, pl.ds(e * half, half)] = high
                    out_ref[rows, pl.ds((3 + e) * half, half)] = high
                    out_ref[rows, pl.ds((6 + e) * half, half)] = low
                    blocks.append((high.astype(F32), low.astype(F32)))
                if out_ref is far_ref:
                    blocks = [h for h, _ in blocks] * 2 + [l for _, l in blocks]
                    for tile in range(last_ref.shape[1] // half):
                        result = jnp.zeros((filters, half), F32)
                        for k, values in enumerate(blocks[tile * X : tile * X + X]):
                            placed = pltpu.roll(values, (k + X - 2) % X * shard, 1)
                            result = jnp.where(slot == k, placed, result)
                        last_ref[rows, pl.ds(tile * half, half)] = result.astype(BF16)


def pack(ref, cells, h, height, row_sets):
    channels, across = ref.shape[0] // height, ref.shape[1]
    lane = lax.broadcasted_iota(jnp.int32, (channels, across), 1)
    middle = ref[pl.ds(h, channels, stride=height), :]
    left = jnp.where(lane == 0, 0.0, pltpu.roll(middle, 1, 1))
    right = jnp.where(lane == across - 1, 0.0, pltpu.roll(middle, across - 1, 1))
    for values, rows in zip((left, middle, right), row_sets):
        high, low = split(values)
        for row, part in zip(rows, (high, low, high)):
            cells[pl.ds(row, channels), pl.ds(h * across, across)] = part


def accumulate(shards, taps_ref, cells, total):
    across = shards[0][0].shape[1]
    height = cells.shape[1] // across
    half = cells.shape[0] // 6
    channels = half // X
    for k, refs in enumerate(shards):
        if not refs:
            for e in range(6):
                rows = pl.ds(e * half + k * channels, channels)
                cells[rows, :] = jnp.zeros((channels, cells.shape[1]), BF16)
    for start in range(0, height, ROWS):
        for h in range(start, start + ROWS):
            for k, refs in enumerate(shards):
                for j, ref in enumerate(refs):
                    row = k * channels + j * channels // len(refs)
                    pack(ref, cells, h, height, [(e * half + row, (3 + e) * half + row) for e in range(3)])
        wide = pl.ds(start * across, ROWS * across)
        products = jnp.dot(
            taps_ref[:, : 6 * half], cells[:, wide], preferred_element_type=F32
        ) + jnp.dot(
            taps_ref[:, 6 * half :], cells[: 3 * half, wide], preferred_element_type=F32
        )
        scatter(products, total, total.shape[0] // 3, start, across)


def scatter(products, total, filters, start, across):
    for a in range(total.shape[0] // filters):
        for b in range(3):
            row = (a * 3 + b) * filters
            place = pl.ds((start + 2 - b) * across, ROWS * across)
            total[pl.ds(a * filters, filters), place] += products[row : row + filters]


def near_kernel(s0, s1, s3, s2a, s2b, taps_ref, total, cells):
    total[...] = jnp.zeros_like(total)
    accumulate(((s0,), (s1,), (s2a, s2b), (s3,)), taps_ref, cells, total)


def far_kernel(s0, s1a, s1b, s3b, s3a, taps_ref, near_ref, total, cells):
    total[...] = near_ref[...]
    accumulate(((s0,), (s1a, s1b), (), (s3a, s3b)), taps_ref, cells, total)


def last_kernel(planes, s2a, s2b, taps_ref, before_ref, *rest):
    *out_refs, cells, total = rest
    across = s2a.shape[1]
    height = cells.shape[1] // across
    part = s2a.shape[0] // height
    channels = 2 * part
    filters = before_ref.shape[0] // 3
    first = planes[0] * filters
    total[...] = before_ref[pl.ds(first, total.shape[0]), :]
    unused = cells.shape[0] - 9 * channels
    cells[pl.ds(9 * channels, unused), :] = jnp.zeros((unused, cells.shape[1]), BF16)
    for start in range(0, height, ROWS):
        for h in range(start, start + ROWS):
            for j, ref in enumerate((s2a, s2b)):
                rows = [[(3 * t + e) * channels + j * part for t in range(3)] for e in range(3)]
                pack(ref, cells, h, height, rows)
        products = jnp.dot(
            taps_ref[pl.ds(3 * first, 3 * total.shape[0]), :],
            cells[:, pl.ds(start * across, ROWS * across)],
            preferred_element_type=F32,
        )
        scatter(products, total, filters, start, across)
    depth = lax.axis_index("depth")
    edge = (depth == 0) | (depth == lax.axis_size("depth") - 1)
    for a, out_ref in enumerate(out_refs):
        for h in range(height):
            values = total[pl.ds(a * filters, filters), pl.ds((h + 1) * across, across)]
            if planes[a] == 0:
                values = jnp.where(edge, 0.0, values)
            out_ref[pl.ds(h, filters, stride=height), :] = values


def divide_kernel(whole_ref, order_ref, low_ref, high_ref):
    low_ref[...] = whole_ref[: low_ref.shape[0]]
    high_ref[...] = whole_ref[low_ref.shape[0] :]


def exchange(block, way):
    planes = lax.axis_size("depth")
    pairs = []
    for c in range(2 * X):
        for d in range(planes):
            step = way if d % 2 else -way
            pairs.append((c * planes + d, (c // X * X + (c + step) % X) * planes + d))
    return lax.ppermute(block, ("chan", "depth"), pairs)


def half_kernel(low, whole_ref, out_ref):
    out_ref[...] = whole_ref[pl.ds(0 if low else out_ref.shape[0], out_ref.shape[0]), :]


def half(whole, low):
    return pl.pallas_call(
        functools.partial(half_kernel, low),
        out_shape=jax.ShapeDtypeStruct((whole.shape[0] // 2, whole.shape[1]), F32),
        compiler_params=LIMIT,
        name="half",
    )(whole)


def spread_own(whole):
    s1, s3 = exchange(whole, 1), exchange(whole, -1)
    return s1, s3, exchange(half(s1, True), 1), exchange(half(s3, False), -1)


def spread(whole, order):
    part = jax.ShapeDtypeStruct((whole.shape[0] // 2, whole.shape[1]), F32)
    low, high = pl.pallas_call(
        divide_kernel,
        out_shape=(part, part),
        in_specs=[pl.BlockSpec(memory_space=pltpu.VMEM), pl.BlockSpec(memory_space=pl.ANY)],
        compiler_params=LIMIT,
        name="divide",
    )(whole, order)
    s1a, s3b = exchange(low, 1), exchange(high, -1)
    s1b, s3a = exchange(high, 1), exchange(low, -1)
    return s1a, s1b, s3b, s3a, exchange(s1a, 1), exchange(s3b, -1)


def local(volume, kernel):
    filters, channels = kernel.shape[3], kernel.shape[4]
    shard, _, height, across = volume.shape
    half = channels // 2
    cells = shard * height
    own = volume.reshape(cells, across)
    other = lax.ppermute(own, "chan", [(i, (i + X) % (2 * X)) for i in range(2 * X)])
    weights = jax.ShapeDtypeStruct((9 * filters, 9 * half), BF16)
    last_weights = jax.ShapeDtypeStruct((9 * filters, 3 * half), BF16)
    near_taps, far_taps, last_taps = pl.pallas_call(
        taps_kernel,
        out_shape=(weights, weights, last_weights),
        compiler_params=LIMIT,
        cost_estimate=pl.CostEstimate(flops=0, bytes_accessed=4_000_000, transcendentals=0),
        name="taps",
    )(kernel)

    def work(planes, part):
        return pl.CostEstimate(
            flops=int(2 * 3 * planes * filters * 9 * half * part * height * across),
            bytes_accessed=3_000_000,
            transcendentals=0,
        )

    total = jax.ShapeDtypeStruct((3 * filters, (height + 2) * across), F32)
    packed = pltpu.VMEM((6 * half, height * across), BF16)
    before = pl.pallas_call(
        near_kernel,
        out_shape=total,
        scratch_shapes=[packed],
        compiler_params=LIMIT,
        cost_estimate=work(3, 1),
        name="near",
    )(own, *spread_own(own), near_taps)
    *most, t2a, t2b = spread(other, before)
    before = pl.pallas_call(
        far_kernel,
        out_shape=total,
        scratch_shapes=[packed],
        compiler_params=LIMIT,
        cost_estimate=work(3, 1),
        name="far",
    )(other, *most, far_taps, before)

    def last(name, *taps):
        part = jax.ShapeDtypeStruct((filters * height, across), F32)
        return pl.pallas_call(
            functools.partial(last_kernel, taps),
            out_shape=[part] * len(taps),
            scratch_shapes=[
                pltpu.VMEM((3 * half, height * across), BF16),
                pltpu.VMEM((len(taps) * filters, total.shape[1]), F32),
            ],
            compiler_params=LIMIT,
            cost_estimate=work(len(taps), 0.25),
            name=name,
        )(t2a, t2b, last_taps, before)

    (off,) = last("off", 0)
    on, mid = last("rest", 1, 2)
    planes = lax.axis_size("depth")
    between = [(i, i + 1) for i in range(1, planes - 1, 2)]
    within = [(i, i + 1) for i in range(0, planes, 2)]
    ends = [(0, 0), (planes - 1, planes - 1)]
    off = lax.ppermute(off, "depth", between + [(j, i) for i, j in between] + ends)
    on = lax.ppermute(on, "depth", within + [(j, i) for i, j in within])
    return (mid + off + on).reshape(filters, 1, height, across)


def solution(mesh):
    return jax.shard_map(
        local,
        mesh=mesh,
        in_specs=(P("chan", "depth", None, None), P(None, None, None, "chan", None)),
        out_specs=P("chan", "depth", None, None),
        check_vma=False,
    )
```

```python
import functools

import jax
import jax.numpy as jnp
from jax import lax
from jax.experimental import pallas as pl
from jax.experimental.pallas import tpu as pltpu
from jax.sharding import PartitionSpec as P

X = 4
ROWS = 2
LIMIT = pltpu.CompilerParams(vmem_limit_bytes=24 * 1024 * 1024)
F32, BF16 = jnp.float32, jnp.bfloat16


def split(values):
    high = values.astype(BF16)
    return high, (values - high.astype(F32)).astype(BF16)


def taps_kernel(kernel_ref, near_ref, far_ref, last_ref):
    me = lax.axis_index("chan")
    core = lax.rem(lax.axis_index("depth"), 2)
    z, x = me // X, lax.rem(me, X)
    filters = kernel_ref.shape[3]
    half = kernel_ref.shape[4] // 2
    shard = half // X
    turn = lax.rem((X - x) * shard, half)
    slot = lax.broadcasted_iota(jnp.int32, (filters, half), 1) // shard
    swapped = ((slot == 1) | (slot == 3)) & (core == 1)
    for out_ref, row in ((near_ref, z), (far_ref, 1 - z)):
        columns = pl.ds(pl.multiple_of(row * half, half), half)
        for a, plane in enumerate((2 - 2 * core, 2 * core, 1)):
            for b in range(3):
                rows = pl.ds((a * 3 + b) * filters, filters)
                blocks = []
                for e in range(3):
                    values = pltpu.roll(kernel_ref[plane, b, e, :, columns], turn, 1)
                    mirrored = pltpu.roll(values, half // 2, 1)
                    high, low = split(jnp.where(swapped, mirrored, values))
                    out_ref[rows, pl.ds(e * half, half)] = high
                    out_ref[rows, pl.ds((3 + e) * half, half)] = high
                    out_ref[rows, pl.ds((6 + e) * half, half)] = low
                    blocks.append((high.astype(F32), low.astype(F32)))
                if out_ref is far_ref:
                    blocks = [h for h, _ in blocks] * 2 + [l for _, l in blocks]
                    for tile in range(last_ref.shape[1] // half):
                        result = jnp.zeros((filters, half), F32)
                        for k, values in enumerate(blocks[tile * X : tile * X + X]):
                            placed = pltpu.roll(values, (k + X - 2) % X * shard, 1)
                            result = jnp.where(slot == k, placed, result)
                        last_ref[rows, pl.ds(tile * half, half)] = result.astype(BF16)


def pack(ref, cells, h, height, row_sets):
    channels, across = ref.shape[0] // height, ref.shape[1]
    lane = lax.broadcasted_iota(jnp.int32, (channels, across), 1)
    middle = ref[pl.ds(h, channels, stride=height), :]
    left = jnp.where(lane == 0, 0.0, pltpu.roll(middle, 1, 1))
    right = jnp.where(lane == across - 1, 0.0, pltpu.roll(middle, across - 1, 1))
    for values, rows in zip((left, middle, right), row_sets):
        high, low = split(values)
        for row, part in zip(rows, (high, low, high)):
            cells[pl.ds(row, channels), pl.ds(h * across, across)] = part


def accumulate(shards, taps_ref, cells, total):
    across = shards[0][0].shape[1]
    height = cells.shape[1] // across
    half = cells.shape[0] // 6
    channels = half // X
    for k, refs in enumerate(shards):
        if not refs:
            for e in range(6):
                rows = pl.ds(e * half + k * channels, channels)
                cells[rows, :] = jnp.zeros((channels, cells.shape[1]), BF16)
    for start in range(0, height, ROWS):
        for h in range(start, start + ROWS):
            for k, refs in enumerate(shards):
                for j, ref in enumerate(refs):
                    row = k * channels + j * channels // len(refs)
                    pack(ref, cells, h, height, [(e * half + row, (3 + e) * half + row) for e in range(3)])
        wide = pl.ds(start * across, ROWS * across)
        products = jnp.dot(
            taps_ref[:, : 6 * half], cells[:, wide], preferred_element_type=F32
        ) + jnp.dot(
            taps_ref[:, 6 * half :], cells[: 3 * half, wide], preferred_element_type=F32
        )
        scatter(products, total, total.shape[0] // 3, start, across)


def scatter(products, total, filters, start, across):
    for a in range(total.shape[0] // filters):
        for b in range(3):
            row = (a * 3 + b) * filters
            place = pl.ds((start + 2 - b) * across, ROWS * across)
            total[pl.ds(a * filters, filters), place] += products[row : row + filters]


def near_kernel(s0, s1, s3, s2a, s2b, taps_ref, total, cells):
    total[...] = jnp.zeros_like(total)
    accumulate(((s0,), (s1,), (s2a, s2b), (s3,)), taps_ref, cells, total)


def far_kernel(s0, s1, s3, taps_ref, near_ref, total, cells):
    total[...] = near_ref[...]
    accumulate(((s0,), (s1,), (), (s3,)), taps_ref, cells, total)


def last_kernel(planes, s2a, s2b, taps_ref, before_ref, *rest):
    *out_refs, cells, total = rest
    across = s2a.shape[1]
    height = cells.shape[1] // across
    part = s2a.shape[0] // height
    channels = 2 * part
    filters = before_ref.shape[0] // 3
    first = planes[0] * filters
    total[...] = before_ref[pl.ds(first, total.shape[0]), :]
    unused = cells.shape[0] - 9 * channels
    cells[pl.ds(9 * channels, unused), :] = jnp.zeros((unused, cells.shape[1]), BF16)
    for start in range(0, height, ROWS):
        for h in range(start, start + ROWS):
            for j, ref in enumerate((s2a, s2b)):
                rows = [[(3 * t + e) * channels + j * part for t in range(3)] for e in range(3)]
                pack(ref, cells, h, height, rows)
        products = jnp.dot(
            taps_ref[pl.ds(3 * first, 3 * total.shape[0]), :],
            cells[:, pl.ds(start * across, ROWS * across)],
            preferred_element_type=F32,
        )
        scatter(products, total, filters, start, across)
    depth = lax.axis_index("depth")
    edge = (depth == 0) | (depth == lax.axis_size("depth") - 1)
    for a, out_ref in enumerate(out_refs):
        for h in range(height):
            values = total[pl.ds(a * filters, filters), pl.ds((h + 1) * across, across)]
            if planes[a] == 0:
                values = jnp.where(edge, 0.0, values)
            out_ref[pl.ds(h, filters, stride=height), :] = values


def exchange(block, way):
    planes = lax.axis_size("depth")
    pairs = []
    for c in range(2 * X):
        for d in range(planes):
            step = way if d % 2 else -way
            pairs.append((c * planes + d, (c // X * X + (c + step) % X) * planes + d))
    return lax.ppermute(block, ("chan", "depth"), pairs)


def half_kernel(low, whole_ref, out_ref):
    out_ref[...] = whole_ref[pl.ds(0 if low else out_ref.shape[0], out_ref.shape[0]), :]


def half(whole, low):
    return pl.pallas_call(
        functools.partial(half_kernel, low),
        out_shape=jax.ShapeDtypeStruct((whole.shape[0] // 2, whole.shape[1]), F32),
        compiler_params=LIMIT,
        name="half",
    )(whole)


def spread(whole):
    s1, s3 = exchange(whole, 1), exchange(whole, -1)
    return s1, s3, exchange(half(s1, True), 1), exchange(half(s3, False), -1)


def local(volume, kernel):
    filters, channels = kernel.shape[3], kernel.shape[4]
    shard, _, height, across = volume.shape
    half = channels // 2
    cells = shard * height
    own = volume.reshape(cells, across)
    other = lax.ppermute(own, "chan", [(i, (i + X) % (2 * X)) for i in range(2 * X)])
    weights = jax.ShapeDtypeStruct((9 * filters, 9 * half), BF16)
    last_weights = jax.ShapeDtypeStruct((9 * filters, 3 * half), BF16)
    near_taps, far_taps, last_taps = pl.pallas_call(
        taps_kernel,
        out_shape=(weights, weights, last_weights),
        compiler_params=LIMIT,
        cost_estimate=pl.CostEstimate(flops=0, bytes_accessed=4_000_000, transcendentals=0),
        name="taps",
    )(kernel)

    def work(planes, part):
        return pl.CostEstimate(
            flops=int(2 * 3 * planes * filters * 9 * half * part * height * across),
            bytes_accessed=3_000_000,
            transcendentals=0,
        )

    total = jax.ShapeDtypeStruct((3 * filters, (height + 2) * across), F32)
    packed = pltpu.VMEM((6 * half, height * across), BF16)
    before = pl.pallas_call(
        near_kernel,
        out_shape=total,
        scratch_shapes=[packed],
        compiler_params=LIMIT,
        cost_estimate=work(3, 4),
        name="near",
    )(own, *spread(own), near_taps)
    *most, t2a, t2b = spread(other)
    before = pl.pallas_call(
        far_kernel,
        out_shape=total,
        scratch_shapes=[packed],
        compiler_params=LIMIT,
        cost_estimate=work(3, 4),
        name="far",
    )(other, *most, far_taps, before)

    def last(name, *taps):
        part = jax.ShapeDtypeStruct((filters * height, across), F32)
        return pl.pallas_call(
            functools.partial(last_kernel, taps),
            out_shape=[part] * len(taps),
            scratch_shapes=[
                pltpu.VMEM((3 * half, height * across), BF16),
                pltpu.VMEM((len(taps) * filters, total.shape[1]), F32),
            ],
            compiler_params=LIMIT,
            cost_estimate=work(len(taps), 0.25),
            name=name,
        )(t2a, t2b, last_taps, before)

    (off,) = last("off", 0)
    on, mid = last("rest", 1, 2)
    planes = lax.axis_size("depth")
    between = [(i, i + 1) for i in range(1, planes - 1, 2)]
    within = [(i, i + 1) for i in range(0, planes, 2)]
    ends = [(0, planes - 1), (planes - 1, 0)]
    off = lax.ppermute(off, "depth", between + [(j, i) for i, j in between] + ends)
    on = lax.ppermute(on, "depth", within + [(j, i) for i, j in within])
    return (mid + off + on).reshape(filters, 1, height, across)


def solution(mesh):
    return jax.shard_map(
        local,
        mesh=mesh,
        in_specs=(P("chan", "depth", None, None), P(None, None, None, "chan", None)),
        out_specs=P("chan", "depth", None, None),
        check_vma=False,
    )
```

```python
import functools

import jax
import jax.numpy as jnp
from jax import lax
from jax.experimental import pallas as pl
from jax.experimental.pallas import tpu as pltpu
from jax.sharding import PartitionSpec as P

X = 4
ROWS = 2
F32, BF16 = jnp.float32, jnp.bfloat16


def split(values):
    high = values.astype(BF16)
    return high, (values - high.astype(F32)).astype(BF16)


def taps_kernel(kernel_ref, near_ref, far_ref, last_ref):
    me = lax.axis_index("chan")
    core = lax.rem(lax.axis_index("depth"), 2)
    z, x = me // X, lax.rem(me, X)
    filters = kernel_ref.shape[3]
    half = kernel_ref.shape[4] // 2
    shard = half // X
    turn = lax.rem((X - x) * shard, half)
    slot = lax.broadcasted_iota(jnp.int32, (filters, half), 1) // shard
    for out_ref, row in ((near_ref, z), (far_ref, 1 - z)):
        columns = pl.ds(pl.multiple_of(row * half, half), half)
        for a, plane in enumerate((2 - 2 * core, 2 * core, 1)):
            for b in range(3):
                rows = pl.ds((a * 3 + b) * filters, filters)
                blocks = []
                for e in range(3):
                    values = pltpu.roll(kernel_ref[plane, b, e, :, columns], turn, 1)
                    high, low = split(values)
                    out_ref[rows, pl.ds(e * half, half)] = high
                    out_ref[rows, pl.ds((3 + e) * half, half)] = high
                    out_ref[rows, pl.ds((6 + e) * half, half)] = low
                    blocks.append((high.astype(F32), low.astype(F32)))
                if out_ref is far_ref:
                    blocks = [h for h, _ in blocks] * 2 + [l for _, l in blocks]
                    for tile in range(last_ref.shape[1] // half):
                        result = jnp.zeros((filters, half), F32)
                        for k, values in enumerate(blocks[tile * X : tile * X + X]):
                            placed = pltpu.roll(values, (k + X - 2) % X * shard, 1)
                            result = jnp.where(slot == k, placed, result)
                        last_ref[rows, pl.ds(tile * half, half)] = result.astype(BF16)


def pack(ref, cells, h, height, row_sets):
    channels, across = ref.shape[0] // height, ref.shape[1]
    lane = lax.broadcasted_iota(jnp.int32, (channels, across), 1)
    middle = ref[pl.ds(h, channels, stride=height), :]
    left = jnp.where(lane == 0, 0.0, pltpu.roll(middle, 1, 1))
    right = jnp.where(lane == across - 1, 0.0, pltpu.roll(middle, across - 1, 1))
    for values, rows in zip((left, middle, right), row_sets):
        high, low = split(values)
        for row, part in zip(rows, (high, low, high)):
            cells[pl.ds(row, channels), pl.ds(h * across, across)] = part


def accumulate(shards, taps_ref, cells, total):
    across = shards[0][0].shape[1]
    height = cells.shape[1] // across
    half = cells.shape[0] // 6
    channels = half // X
    for k, refs in enumerate(shards):
        if not refs:
            for e in range(6):
                rows = pl.ds(e * half + k * channels, channels)
                cells[rows, :] = jnp.zeros((channels, cells.shape[1]), BF16)
    for start in range(0, height, ROWS):
        for h in range(start, start + ROWS):
            for k, refs in enumerate(shards):
                for j, ref in enumerate(refs):
                    row = k * channels + j * channels // len(refs)
                    pack(ref, cells, h, height, [(e * half + row, (3 + e) * half + row) for e in range(3)])
        wide = pl.ds(start * across, ROWS * across)
        products = jnp.dot(
            taps_ref[:, : 6 * half], cells[:, wide], preferred_element_type=F32
        ) + jnp.dot(
            taps_ref[:, 6 * half :], cells[: 3 * half, wide], preferred_element_type=F32
        )
        scatter(products, total, total.shape[0] // 3, start, across)


def scatter(products, total, filters, start, across):
    for a in range(total.shape[0] // filters):
        for b in range(3):
            row = (a * 3 + b) * filters
            place = pl.ds((start + 2 - b) * across, ROWS * across)
            total[pl.ds(a * filters, filters), place] += products[row : row + filters]


def near_kernel(s0, s1, s2, s3, taps_ref, total, cells):
    total[...] = jnp.zeros_like(total)
    accumulate(((s0,), (s1,), (s2,), (s3,)), taps_ref, cells, total)


def far_kernel(s0, s1a, s1b, s3a, s3b, taps_ref, near_ref, total, cells):
    total[...] = near_ref[...]
    accumulate(((s0,), (s1a, s1b), (), (s3a, s3b)), taps_ref, cells, total)


def last_kernel(planes, s2a, s2b, taps_ref, before_ref, *rest):
    *out_refs, cells, total = rest
    across = s2a.shape[1]
    height = cells.shape[1] // across
    part = s2a.shape[0] // height
    channels = 2 * part
    filters = before_ref.shape[0] // 3
    first = planes[0] * filters
    total[...] = before_ref[pl.ds(first, total.shape[0]), :]
    unused = cells.shape[0] - 9 * channels
    cells[pl.ds(9 * channels, unused), :] = jnp.zeros((unused, cells.shape[1]), BF16)
    for start in range(0, height, ROWS):
        for h in range(start, start + ROWS):
            for j, ref in enumerate((s2a, s2b)):
                rows = [[(3 * t + e) * channels + j * part for t in range(3)] for e in range(3)]
                pack(ref, cells, h, height, rows)
        products = jnp.dot(
            taps_ref[pl.ds(3 * first, 3 * total.shape[0]), :],
            cells[:, pl.ds(start * across, ROWS * across)],
            preferred_element_type=F32,
        )
        scatter(products, total, filters, start, across)
    depth = lax.axis_index("depth")
    edge = (depth == 0) | (depth == lax.axis_size("depth") - 1)
    for a, out_ref in enumerate(out_refs):
        for h in range(height):
            values = total[pl.ds(a * filters, filters), pl.ds((h + 1) * across, across)]
            if planes[a] == 0:
                values = jnp.where(edge, 0.0, values)
            out_ref[pl.ds(h, filters, stride=height), :] = values


def from_x(block, step):
    pairs = [(g * X + i, g * X + (i - step) % X) for g in range(2) for i in range(X)]
    return lax.ppermute(block, "chan", pairs)


def divide_kernel(whole_ref, order_ref, low_ref, high_ref):
    low_ref[...] = whole_ref[: low_ref.shape[0]]
    high_ref[...] = whole_ref[low_ref.shape[0] :]


def local(volume, kernel):
    filters, channels = kernel.shape[3], kernel.shape[4]
    shard, _, height, across = volume.shape
    half = channels // 2
    cells = shard * height
    limit = pltpu.CompilerParams(vmem_limit_bytes=24 * 1024 * 1024)
    own = volume.reshape(cells, across)
    other = lax.ppermute(own, "chan", [(i, (i + X) % (2 * X)) for i in range(2 * X)])
    s1, s3, s2 = [from_x(own, step) for step in (1, 3, 2)]
    weights = jax.ShapeDtypeStruct((9 * filters, 9 * half), BF16)
    last_weights = jax.ShapeDtypeStruct((9 * filters, 3 * half), BF16)
    near_taps, far_taps, last_taps = pl.pallas_call(
        taps_kernel,
        out_shape=(weights, weights, last_weights),
        compiler_params=limit,
        cost_estimate=pl.CostEstimate(flops=0, bytes_accessed=4_000_000, transcendentals=0),
        name="taps",
    )(kernel)

    part = jax.ShapeDtypeStruct((cells // 2, across), F32)
    low, high = pl.pallas_call(
        divide_kernel,
        out_shape=(part, part),
        in_specs=[pl.BlockSpec(memory_space=pltpu.VMEM), pl.BlockSpec(memory_space=pl.ANY)],
        compiler_params=limit,
        name="divide",
    )(other, last_taps)
    t3a, t1b = from_x(low, 3), from_x(high, 1)
    t3b, t1a = from_x(high, 3), from_x(low, 1)
    t2a, t2b = from_x(t3a, 3), from_x(t1b, 1)

    def work(planes, part):
        return pl.CostEstimate(
            flops=int(2 * 3 * planes * filters * 9 * half * part * height * across),
            bytes_accessed=3_000_000,
            transcendentals=0,
        )

    total = jax.ShapeDtypeStruct((3 * filters, (height + 2) * across), F32)
    packed = pltpu.VMEM((6 * half, height * across), BF16)
    before = pl.pallas_call(
        near_kernel,
        out_shape=total,
        scratch_shapes=[packed],
        compiler_params=limit,
        cost_estimate=work(3, 1),
        name="near",
    )(own, s1, s2, s3, near_taps)
    before = pl.pallas_call(
        far_kernel,
        out_shape=total,
        scratch_shapes=[packed],
        compiler_params=limit,
        cost_estimate=work(3, 1),
        name="far",
    )(other, t1a, t1b, t3a, t3b, far_taps, before)

    def last(name, *taps):
        part = jax.ShapeDtypeStruct((filters * height, across), F32)
        return pl.pallas_call(
            functools.partial(last_kernel, taps),
            out_shape=[part] * len(taps),
            scratch_shapes=[
                pltpu.VMEM((3 * half, height * across), BF16),
                pltpu.VMEM((len(taps) * filters, total.shape[1]), F32),
            ],
            compiler_params=limit,
            cost_estimate=work(len(taps), 0.25),
            name=name,
        )(t2a, t2b, last_taps, before)

    (off,) = last("off", 0)
    on, mid = last("rest", 1, 2)
    planes = lax.axis_size("depth")
    between = [(i, i + 1) for i in range(1, planes - 1, 2)]
    within = [(i, i + 1) for i in range(0, planes, 2)]
    ends = [(0, planes - 1), (planes - 1, 0)]
    off = lax.ppermute(off, "depth", between + [(j, i) for i, j in between] + ends)
    on = lax.ppermute(on, "depth", within + [(j, i) for i, j in within])
    return (mid + off + on).reshape(filters, 1, height, across)


def solution(mesh):
    return jax.shard_map(
        local,
        mesh=mesh,
        in_specs=(P("chan", "depth", None, None), P(None, None, None, "chan", None)),
        out_specs=P("chan", "depth", None, None),
        check_vma=False,
    )
```

```python
import functools

import jax
import jax.numpy as jnp
from jax import lax
from jax.experimental import pallas as pl
from jax.experimental.pallas import tpu as pltpu
from jax.sharding import PartitionSpec as P

X = 4
ROWS = 2
F32, BF16 = jnp.float32, jnp.bfloat16


def split(values):
    high = values.astype(BF16)
    return high, (values - high.astype(F32)).astype(BF16)


def taps_kernel(kernel_ref, near_ref, far_ref, last_ref):
    me = lax.axis_index("chan")
    core = lax.rem(lax.axis_index("depth"), 2)
    z, x = me // X, lax.rem(me, X)
    filters = kernel_ref.shape[3]
    half = kernel_ref.shape[4] // 2
    shard = half // X
    turn = lax.rem((X - x) * shard, half)
    slot = lax.broadcasted_iota(jnp.int32, (filters, half), 1) // shard
    for out_ref, row in ((near_ref, z), (far_ref, 1 - z)):
        columns = pl.ds(pl.multiple_of(row * half, half), half)
        for a, plane in enumerate((2 - 2 * core, 2 * core, 1)):
            for b in range(3):
                rows = pl.ds((a * 3 + b) * filters, filters)
                blocks = []
                for e in range(3):
                    values = pltpu.roll(kernel_ref[plane, b, e, :, columns], turn, 1)
                    high, low = split(values)
                    out_ref[rows, pl.ds(e * half, half)] = high
                    out_ref[rows, pl.ds((3 + e) * half, half)] = high
                    out_ref[rows, pl.ds((6 + e) * half, half)] = low
                    blocks.append((high.astype(F32), low.astype(F32)))
                if out_ref is far_ref:
                    blocks = [h for h, _ in blocks] * 2 + [l for _, l in blocks]
                    for tile in range(last_ref.shape[1] // half):
                        result = jnp.zeros((filters, half), F32)
                        for k, values in enumerate(blocks[tile * X : tile * X + X]):
                            placed = pltpu.roll(values, (k + X - 2) % X * shard, 1)
                            result = jnp.where(slot == k, placed, result)
                        last_ref[rows, pl.ds(tile * half, half)] = result.astype(BF16)


def pack(ref, cells, h, height, row_sets):
    channels, across = ref.shape[0] // height, ref.shape[1]
    lane = lax.broadcasted_iota(jnp.int32, (channels, across), 1)
    middle = ref[pl.ds(h, channels, stride=height), :]
    left = jnp.where(lane == 0, 0.0, pltpu.roll(middle, 1, 1))
    right = jnp.where(lane == across - 1, 0.0, pltpu.roll(middle, across - 1, 1))
    for values, rows in zip((left, middle, right), row_sets):
        high, low = split(values)
        for row, part in zip(rows, (high, low, high)):
            cells[pl.ds(row, channels), pl.ds(h * across, across)] = part


def accumulate(shards, taps_ref, cells, total):
    across = shards[0][0].shape[1]
    height = cells.shape[1] // across
    half = cells.shape[0] // 6
    channels = half // X
    for k, refs in enumerate(shards):
        if not refs:
            for e in range(6):
                rows = pl.ds(e * half + k * channels, channels)
                cells[rows, :] = jnp.zeros((channels, cells.shape[1]), BF16)
    for start in range(0, height, ROWS):
        for h in range(start, start + ROWS):
            for k, refs in enumerate(shards):
                for j, ref in enumerate(refs):
                    row = k * channels + j * channels // len(refs)
                    pack(ref, cells, h, height, [(e * half + row, (3 + e) * half + row) for e in range(3)])
        wide = pl.ds(start * across, ROWS * across)
        products = jnp.dot(
            taps_ref[:, : 6 * half], cells[:, wide], preferred_element_type=F32
        ) + jnp.dot(
            taps_ref[:, 6 * half :], cells[: 3 * half, wide], preferred_element_type=F32
        )
        scatter(products, total, total.shape[0] // 3, start, across)


def scatter(products, total, filters, start, across):
    for a in range(total.shape[0] // filters):
        for b in range(3):
            row = (a * 3 + b) * filters
            place = pl.ds((start + 2 - b) * across, ROWS * across)
            total[pl.ds(a * filters, filters), place] += products[row : row + filters]


def near_kernel(s0, s1, s2, s3, taps_ref, total, cells):
    total[...] = jnp.zeros_like(total)
    accumulate(((s0,), (s1,), (s2,), (s3,)), taps_ref, cells, total)


def far_kernel(s0, s1a, s1b, s3a, s3b, taps_ref, near_ref, total, cells):
    total[...] = near_ref[...]
    accumulate(((s0,), (s1a, s1b), (), (s3a, s3b)), taps_ref, cells, total)


def last_kernel(planes, s2a, s2b, taps_ref, before_ref, *rest):
    *out_refs, cells, total = rest
    across = s2a.shape[1]
    height = cells.shape[1] // across
    part = s2a.shape[0] // height
    channels = 2 * part
    filters = before_ref.shape[0] // 3
    first = planes[0] * filters
    total[...] = before_ref[pl.ds(first, total.shape[0]), :]
    unused = cells.shape[0] - 9 * channels
    cells[pl.ds(9 * channels, unused), :] = jnp.zeros((unused, cells.shape[1]), BF16)
    for start in range(0, height, ROWS):
        for h in range(start, start + ROWS):
            for j, ref in enumerate((s2a, s2b)):
                rows = [[(3 * t + e) * channels + j * part for t in range(3)] for e in range(3)]
                pack(ref, cells, h, height, rows)
        products = jnp.dot(
            taps_ref[pl.ds(3 * first, 3 * total.shape[0]), :],
            cells[:, pl.ds(start * across, ROWS * across)],
            preferred_element_type=F32,
        )
        scatter(products, total, filters, start, across)
    depth = lax.axis_index("depth")
    edge = (depth == 0) | (depth == lax.axis_size("depth") - 1)
    for a, out_ref in enumerate(out_refs):
        for h in range(height):
            values = total[pl.ds(a * filters, filters), pl.ds((h + 1) * across, across)]
            if planes[a] == 0:
                values = jnp.where(edge, 0.0, values)
            out_ref[pl.ds(h, filters, stride=height), :] = values


def from_x(block, step):
    pairs = [(g * X + i, g * X + (i - step) % X) for g in range(2) for i in range(X)]
    return lax.ppermute(block, "chan", pairs)


def divide_kernel(whole_ref, order_ref, low_ref, high_ref):
    low_ref[...] = whole_ref[: low_ref.shape[0]]
    high_ref[...] = whole_ref[low_ref.shape[0] :]


def local(volume, kernel):
    filters, channels = kernel.shape[3], kernel.shape[4]
    shard, _, height, across = volume.shape
    half = channels // 2
    cells = shard * height
    limit = pltpu.CompilerParams(vmem_limit_bytes=24 * 1024 * 1024)
    own = volume.reshape(cells, across)
    other = lax.ppermute(own, "chan", [(i, (i + X) % (2 * X)) for i in range(2 * X)])
    s1, s3, s2 = [from_x(own, step) for step in (1, 3, 2)]
    weights = jax.ShapeDtypeStruct((9 * filters, 9 * half), BF16)
    last_weights = jax.ShapeDtypeStruct((9 * filters, 3 * half), BF16)
    near_taps, far_taps, last_taps = pl.pallas_call(
        taps_kernel,
        out_shape=(weights, weights, last_weights),
        compiler_params=limit,
        cost_estimate=pl.CostEstimate(flops=0, bytes_accessed=4_000_000, transcendentals=0),
        name="taps",
    )(kernel)

    part = jax.ShapeDtypeStruct((cells // 2, across), F32)
    low, high = pl.pallas_call(
        divide_kernel,
        out_shape=(part, part),
        in_specs=[pl.BlockSpec(memory_space=pltpu.VMEM), pl.BlockSpec(memory_space=pl.ANY)],
        compiler_params=limit,
        name="divide",
    )(other, last_taps)
    t3a, t1b = from_x(low, 3), from_x(high, 1)
    t3b, t1a = from_x(high, 3), from_x(low, 1)
    t2a, t2b = from_x(t3a, 3), from_x(t1b, 1)

    def work(planes, part):
        return pl.CostEstimate(
            flops=int(2 * 3 * planes * filters * 9 * half * part * height * across),
            bytes_accessed=3_000_000,
            transcendentals=0,
        )

    total = jax.ShapeDtypeStruct((3 * filters, (height + 2) * across), F32)
    packed = pltpu.VMEM((6 * half, height * across), BF16)
    before = pl.pallas_call(
        near_kernel,
        out_shape=total,
        scratch_shapes=[packed],
        compiler_params=limit,
        cost_estimate=work(3, 1),
        name="near",
    )(own, s1, s2, s3, near_taps)
    before = pl.pallas_call(
        far_kernel,
        out_shape=total,
        scratch_shapes=[packed],
        compiler_params=limit,
        cost_estimate=work(3, 1),
        name="far",
    )(other, t1a, t1b, t3a, t3b, far_taps, before)

    def last(name, *taps):
        part = jax.ShapeDtypeStruct((filters * height, across), F32)
        return pl.pallas_call(
            functools.partial(last_kernel, taps),
            out_shape=[part] * len(taps),
            scratch_shapes=[
                pltpu.VMEM((3 * half, height * across), BF16),
                pltpu.VMEM((len(taps) * filters, total.shape[1]), F32),
            ],
            compiler_params=limit,
            cost_estimate=work(len(taps), 0.25),
            name=name,
        )(t2a, t2b, last_taps, before)

    (off,) = last("off", 0)
    on, mid = last("rest", 1, 2)
    planes = lax.axis_size("depth")
    between = [(i, i + 1) for i in range(1, planes - 1, 2)]
    within = [(i, i + 1) for i in range(0, planes, 2)]
    pairs = []
    for c in range(2 * X):
        pairs += [(c * planes + i, c * planes + j) for k, l in between for i, j in ((k, l), (l, k))]
        pairs += [(c * planes + d, (c ^ 1) * planes + d) for d in (0, planes - 1)]
    off = lax.ppermute(off, ("chan", "depth"), pairs)
    on = lax.ppermute(on, "depth", within + [(j, i) for i, j in within])
    return (mid + off + on).reshape(filters, 1, height, across)


def solution(mesh):
    return jax.shard_map(
        local,
        mesh=mesh,
        in_specs=(P("chan", "depth", None, None), P(None, None, None, "chan", None)),
        out_specs=P("chan", "depth", None, None),
        check_vma=False,
    )
```

```python
import functools

import jax
import jax.numpy as jnp
from jax import lax
from jax.experimental import pallas as pl
from jax.experimental.pallas import tpu as pltpu
from jax.sharding import PartitionSpec as P

X = 4
ROWS = 2
LIMIT = pltpu.CompilerParams(vmem_limit_bytes=24 * 1024 * 1024)
F32, BF16 = jnp.float32, jnp.bfloat16


def split(values):
    high = values.astype(BF16)
    return high, (values - high.astype(F32)).astype(BF16)


def taps_kernel(kernel_ref, near_ref, far_ref, last_ref):
    me = lax.axis_index("chan")
    core = lax.rem(lax.axis_index("depth"), 2)
    z, x = me // X, lax.rem(me, X)
    filters = kernel_ref.shape[3]
    half = kernel_ref.shape[4] // 2
    shard = half // X
    turn = lax.rem((X - x) * shard, half)
    unit = lax.broadcasted_iota(jnp.int32, (filters, half), 1) // (shard // 2)
    for out_ref, row in ((near_ref, z), (far_ref, 1 - z)):
        columns = pl.ds(pl.multiple_of(row * half, half), half)
        for a, plane in enumerate((2 - 2 * core, 2 * core, 1)):
            for b in range(3):
                rows = pl.ds((a * 3 + b) * filters, filters)
                blocks = []
                for e in range(3):
                    values = pltpu.roll(kernel_ref[plane, b, e, :, columns], turn, 1)
                    high, low = split(values)
                    out_ref[rows, pl.ds(e * half, half)] = high
                    out_ref[rows, pl.ds((3 + e) * half, half)] = high
                    out_ref[rows, pl.ds((6 + e) * half, half)] = low
                    blocks.append((high.astype(F32), low.astype(F32)))
                if out_ref is far_ref:
                    blocks = [h for h, _ in blocks] * 2 + [l for _, l in blocks]
                    for tile in range(last_ref.shape[1] // half):
                        result = jnp.zeros((filters, half), F32)
                        for k, values in enumerate(blocks[tile * X : tile * X + X]):
                            low = pltpu.roll(values, (k + X - 1) % X * shard, 1)
                            high = pltpu.roll(values, (k + X - 3) % X * shard, 1)
                            result = jnp.where(unit == 2 * k, low, result)
                            result = jnp.where(unit == 2 * k + 1, high, result)
                        last_ref[rows, pl.ds(tile * half, half)] = result.astype(BF16)


def pack(ref, cells, h, height, row_sets):
    channels, across = ref.shape[0] // height, ref.shape[1]
    lane = lax.broadcasted_iota(jnp.int32, (channels, across), 1)
    middle = ref[pl.ds(h, channels, stride=height), :]
    left = jnp.where(lane == 0, 0.0, pltpu.roll(middle, 1, 1))
    right = jnp.where(lane == across - 1, 0.0, pltpu.roll(middle, across - 1, 1))
    for values, rows in zip((left, middle, right), row_sets):
        high, low = split(values)
        for row, part in zip(rows, (high, low, high)):
            cells[pl.ds(row, channels), pl.ds(h * across, across)] = part


def accumulate(shards, unused, taps_ref, cells, total):
    across = shards[0][0].shape[1]
    height = cells.shape[1] // across
    half = cells.shape[0] // 6
    for place, channels in unused:
        for e in range(6):
            cells[pl.ds(e * half + place, channels), :] = jnp.zeros((channels, cells.shape[1]), BF16)
    for start in range(0, height, ROWS):
        for h in range(start, start + ROWS):
            for ref, place in shards:
                rows = [(e * half + place, (3 + e) * half + place) for e in range(3)]
                pack(ref, cells, h, height, rows)
        wide = pl.ds(start * across, ROWS * across)
        products = jnp.dot(
            taps_ref[:, : 6 * half], cells[:, wide], preferred_element_type=F32
        ) + jnp.dot(
            taps_ref[:, 6 * half :], cells[: 3 * half, wide], preferred_element_type=F32
        )
        scatter(products, total, total.shape[0] // 3, start, across)


def scatter(products, total, filters, start, across):
    for a in range(total.shape[0] // filters):
        for b in range(3):
            row = (a * 3 + b) * filters
            place = pl.ds((start + 2 - b) * across, ROWS * across)
            total[pl.ds(a * filters, filters), place] += products[row : row + filters]


def near_kernel(s0, s1, s2, s3, taps_ref, total, cells):
    n = taps_ref.shape[1] // 9 // X
    total[...] = jnp.zeros_like(total)
    accumulate(((s0, 0), (s1, n), (s2, 2 * n), (s3, 3 * n)), (), taps_ref, cells, total)


def far_kernel(s0, s1b, s2a, s2b, s3a, taps_ref, near_ref, total, cells):
    n = taps_ref.shape[1] // 9 // X
    m = n // 2
    total[...] = near_ref[...]
    accumulate(
        ((s0, 0), (s1b, n + m), (s2a, 2 * n), (s2b, 2 * n + m), (s3a, 3 * n)),
        ((n, m), (3 * n + m, m)),
        taps_ref,
        cells,
        total,
    )


def last_kernel(planes, low, high, taps_ref, before_ref, *rest):
    *out_refs, cells, total = rest
    across = low.shape[1]
    height = cells.shape[1] // across
    part = low.shape[0] // height
    channels = 2 * part
    filters = before_ref.shape[0] // 3
    first = planes[0] * filters
    total[...] = before_ref[pl.ds(first, total.shape[0]), :]
    unused = cells.shape[0] - 9 * channels
    cells[pl.ds(9 * channels, unused), :] = jnp.zeros((unused, cells.shape[1]), BF16)
    for start in range(0, height, ROWS):
        for h in range(start, start + ROWS):
            for j, ref in enumerate((low, high)):
                rows = [[(3 * t + e) * channels + j * part for t in range(3)] for e in range(3)]
                pack(ref, cells, h, height, rows)
        products = jnp.dot(
            taps_ref[pl.ds(3 * first, 3 * total.shape[0]), :],
            cells[:, pl.ds(start * across, ROWS * across)],
            preferred_element_type=F32,
        )
        scatter(products, total, filters, start, across)
    depth = lax.axis_index("depth")
    edge = (depth == 0) | (depth == lax.axis_size("depth") - 1)
    for a, out_ref in enumerate(out_refs):
        for h in range(height):
            values = total[pl.ds(a * filters, filters), pl.ds((h + 1) * across, across)]
            if planes[a] == 0:
                values = jnp.where(edge, 0.0, values)
            out_ref[pl.ds(h, filters, stride=height), :] = values


def from_x(block, step):
    pairs = [(g * X + i, g * X + (i - step) % X) for g in range(2) for i in range(X)]
    return lax.ppermute(block, "chan", pairs)


def divide_kernel(whole_ref, order_ref, low_ref, high_ref):
    low_ref[...] = whole_ref[: low_ref.shape[0]]
    high_ref[...] = whole_ref[low_ref.shape[0] :]


def copy_kernel(one_ref, order_ref, out_ref):
    out_ref[...] = one_ref[...]


def behind(one, order):
    return pl.pallas_call(
        copy_kernel,
        out_shape=jax.ShapeDtypeStruct(one.shape, one.dtype),
        in_specs=[pl.BlockSpec(memory_space=pltpu.VMEM), pl.BlockSpec(memory_space=pl.ANY)],
        compiler_params=LIMIT,
        name="behind",
    )(one, order)


def local(volume, kernel):
    filters, channels = kernel.shape[3], kernel.shape[4]
    shard, _, height, across = volume.shape
    half = channels // 2
    cells = shard * height
    own = volume.reshape(cells, across)
    other = lax.ppermute(own, "chan", [(i, (i + X) % (2 * X)) for i in range(2 * X)])
    s1, s3, s2 = [from_x(own, step) for step in (1, 3, 2)]
    weights = jax.ShapeDtypeStruct((9 * filters, 9 * half), BF16)
    last_weights = jax.ShapeDtypeStruct((9 * filters, 3 * half), BF16)
    near_taps, far_taps, last_taps = pl.pallas_call(
        taps_kernel,
        out_shape=(weights, weights, last_weights),
        compiler_params=LIMIT,
        cost_estimate=pl.CostEstimate(flops=0, bytes_accessed=4_000_000, transcendentals=0),
        name="taps",
    )(kernel)

    part = jax.ShapeDtypeStruct((cells // 2, across), F32)
    low, high = pl.pallas_call(
        divide_kernel,
        out_shape=(part, part),
        in_specs=[pl.BlockSpec(memory_space=pltpu.VMEM), pl.BlockSpec(memory_space=pl.ANY)],
        compiler_params=LIMIT,
        name="divide",
    )(other, last_taps)
    t3a, t1b = from_x(low, 3), from_x(high, 1)
    t2a, t2b = from_x(t3a, 3), from_x(t1b, 1)
    t3b, t1a = from_x(behind(high, t1b), 3), from_x(behind(low, t3a), 1)

    def work(planes, part):
        return pl.CostEstimate(
            flops=int(2 * 3 * planes * filters * 9 * half * part * height * across),
            bytes_accessed=3_000_000,
            transcendentals=0,
        )

    total = jax.ShapeDtypeStruct((3 * filters, (height + 2) * across), F32)
    packed = pltpu.VMEM((6 * half, height * across), BF16)
    before = pl.pallas_call(
        near_kernel,
        out_shape=total,
        scratch_shapes=[packed],
        compiler_params=LIMIT,
        cost_estimate=work(3, 1),
        name="near",
    )(own, s1, s2, s3, near_taps)
    before = pl.pallas_call(
        far_kernel,
        out_shape=total,
        scratch_shapes=[packed],
        compiler_params=LIMIT,
        cost_estimate=work(3, 1),
        name="far",
    )(other, t1b, t2a, t2b, t3a, far_taps, before)

    def last(name, *taps):
        part = jax.ShapeDtypeStruct((filters * height, across), F32)
        return pl.pallas_call(
            functools.partial(last_kernel, taps),
            out_shape=[part] * len(taps),
            scratch_shapes=[
                pltpu.VMEM((3 * half, height * across), BF16),
                pltpu.VMEM((len(taps) * filters, total.shape[1]), F32),
            ],
            compiler_params=LIMIT,
            cost_estimate=work(len(taps), 0.25),
            name=name,
        )(t1a, t3b, last_taps, before)

    off, on, mid = last("last", 0, 1, 2)
    planes = lax.axis_size("depth")
    between = [(i, i + 1) for i in range(1, planes - 1, 2)]
    within = [(i, i + 1) for i in range(0, planes, 2)]
    pairs = []
    for c in range(2 * X):
        pairs += [(c * planes + i, c * planes + j) for k, l in between for i, j in ((k, l), (l, k))]
        pairs += [(c * planes + d, (c ^ 1) * planes + d) for d in (0, planes - 1)]
    off = lax.ppermute(off, ("chan", "depth"), pairs)
    on = lax.ppermute(on, "depth", within + [(j, i) for i, j in within])
    return (mid + off + on).reshape(filters, 1, height, across)


def solution(mesh):
    return jax.shard_map(
        local,
        mesh=mesh,
        in_specs=(P("chan", "depth", None, None), P(None, None, None, "chan", None)),
        out_specs=P("chan", "depth", None, None),
        check_vma=False,
    )
```

```python
import functools

import jax
import jax.numpy as jnp
from jax import lax
from jax.experimental import pallas as pl
from jax.experimental.pallas import tpu as pltpu
from jax.sharding import PartitionSpec as P

X = 4
ROWS = 2
LIMIT = pltpu.CompilerParams(vmem_limit_bytes=24 * 1024 * 1024)
F32, BF16 = jnp.float32, jnp.bfloat16


def split(values):
    high = values.astype(BF16)
    return high, (values - high.astype(F32)).astype(BF16)


def taps_kernel(kernel_ref, near_ref, far_ref, last_ref):
    me = lax.axis_index("chan")
    core = lax.rem(lax.axis_index("depth"), 2)
    z, x = me // X, lax.rem(me, X)
    filters = kernel_ref.shape[3]
    half = kernel_ref.shape[4] // 2
    shard = half // X
    turn = lax.rem((X - x) * shard, half)
    unit = lax.broadcasted_iota(jnp.int32, (filters, half), 1) // (shard // 2)
    for out_ref, row in ((near_ref, z), (far_ref, 1 - z)):
        columns = pl.ds(pl.multiple_of(row * half, half), half)
        for a, plane in enumerate((2 - 2 * core, 2 * core, 1)):
            for b in range(3):
                rows = pl.ds((a * 3 + b) * filters, filters)
                blocks = []
                for e in range(3):
                    values = pltpu.roll(kernel_ref[plane, b, e, :, columns], turn, 1)
                    high, low = split(values)
                    out_ref[rows, pl.ds(e * half, half)] = high
                    out_ref[rows, pl.ds((3 + e) * half, half)] = high
                    out_ref[rows, pl.ds((6 + e) * half, half)] = low
                    blocks.append((high.astype(F32), low.astype(F32)))
                if out_ref is far_ref:
                    blocks = [h for h, _ in blocks] * 2 + [l for _, l in blocks]
                    for tile in range(last_ref.shape[1] // half):
                        result = jnp.zeros((filters, half), F32)
                        for k, values in enumerate(blocks[tile * X : tile * X + X]):
                            low = pltpu.roll(values, (k + X - 1) % X * shard, 1)
                            high = pltpu.roll(values, (k + X - 3) % X * shard, 1)
                            result = jnp.where(unit == 2 * k, low, result)
                            result = jnp.where(unit == 2 * k + 1, high, result)
                        last_ref[rows, pl.ds(tile * half, half)] = result.astype(BF16)


def pack(ref, cells, h, height, row_sets):
    channels, across = ref.shape[0] // height, ref.shape[1]
    lane = lax.broadcasted_iota(jnp.int32, (channels, across), 1)
    middle = ref[pl.ds(h, channels, stride=height), :]
    left = jnp.where(lane == 0, 0.0, pltpu.roll(middle, 1, 1))
    right = jnp.where(lane == across - 1, 0.0, pltpu.roll(middle, across - 1, 1))
    for values, rows in zip((left, middle, right), row_sets):
        high, low = split(values)
        for row, part in zip(rows, (high, low, high)):
            cells[pl.ds(row, channels), pl.ds(h * across, across)] = part


def accumulate(shards, unused, taps_ref, cells, total):
    across = shards[0][0].shape[1]
    height = cells.shape[1] // across
    half = cells.shape[0] // 6
    for place, channels in unused:
        for e in range(6):
            cells[pl.ds(e * half + place, channels), :] = jnp.zeros((channels, cells.shape[1]), BF16)
    for start in range(0, height, ROWS):
        for h in range(start, start + ROWS):
            for ref, place in shards:
                rows = [(e * half + place, (3 + e) * half + place) for e in range(3)]
                pack(ref, cells, h, height, rows)
        wide = pl.ds(start * across, ROWS * across)
        products = jnp.dot(
            taps_ref[:, : 6 * half], cells[:, wide], preferred_element_type=F32
        ) + jnp.dot(
            taps_ref[:, 6 * half :], cells[: 3 * half, wide], preferred_element_type=F32
        )
        scatter(products, total, total.shape[0] // 3, start, across)


def scatter(products, total, filters, start, across):
    for a in range(total.shape[0] // filters):
        for b in range(3):
            row = (a * 3 + b) * filters
            place = pl.ds((start + 2 - b) * across, ROWS * across)
            total[pl.ds(a * filters, filters), place] += products[row : row + filters]


def near_kernel(s0, s1, s2, s3, taps_ref, total, cells):
    n = taps_ref.shape[1] // 9 // X
    total[...] = jnp.zeros_like(total)
    accumulate(((s0, 0), (s1, n), (s2, 2 * n), (s3, 3 * n)), (), taps_ref, cells, total)


def far_kernel(s0, s1b, s2a, s2b, s3a, taps_ref, near_ref, total, cells):
    n = taps_ref.shape[1] // 9 // X
    m = n // 2
    total[...] = near_ref[...]
    accumulate(
        ((s0, 0), (s1b, n + m), (s2a, 2 * n), (s2b, 2 * n + m), (s3a, 3 * n)),
        ((n, m), (3 * n + m, m)),
        taps_ref,
        cells,
        total,
    )


def last_kernel(planes, low, high, taps_ref, before_ref, *rest):
    *out_refs, cells, total = rest
    across = low.shape[1]
    height = cells.shape[1] // across
    part = low.shape[0] // height
    channels = 2 * part
    filters = before_ref.shape[0] // 3
    first = planes[0] * filters
    total[...] = before_ref[pl.ds(first, total.shape[0]), :]
    unused = cells.shape[0] - 9 * channels
    cells[pl.ds(9 * channels, unused), :] = jnp.zeros((unused, cells.shape[1]), BF16)
    for start in range(0, height, ROWS):
        for h in range(start, start + ROWS):
            for j, ref in enumerate((low, high)):
                rows = [[(3 * t + e) * channels + j * part for t in range(3)] for e in range(3)]
                pack(ref, cells, h, height, rows)
        products = jnp.dot(
            taps_ref[pl.ds(3 * first, 3 * total.shape[0]), :],
            cells[:, pl.ds(start * across, ROWS * across)],
            preferred_element_type=F32,
        )
        scatter(products, total, filters, start, across)
    depth = lax.axis_index("depth")
    edge = (depth == 0) | (depth == lax.axis_size("depth") - 1)
    for a, out_ref in enumerate(out_refs):
        for h in range(height):
            values = total[pl.ds(a * filters, filters), pl.ds((h + 1) * across, across)]
            if planes[a] == 0:
                values = jnp.where(edge, 0.0, values)
            out_ref[pl.ds(h, filters, stride=height), :] = values


def from_x(block, step):
    pairs = [(g * X + i, g * X + (i - step) % X) for g in range(2) for i in range(X)]
    return lax.ppermute(block, "chan", pairs)


def divide_kernel(whole_ref, order_ref, low_ref, high_ref):
    low_ref[...] = whole_ref[: low_ref.shape[0]]
    high_ref[...] = whole_ref[low_ref.shape[0] :]


def copy_kernel(one_ref, order_ref, out_ref):
    out_ref[...] = one_ref[...]


def behind(one, order):
    return pl.pallas_call(
        copy_kernel,
        out_shape=jax.ShapeDtypeStruct(one.shape, one.dtype),
        in_specs=[pl.BlockSpec(memory_space=pltpu.VMEM), pl.BlockSpec(memory_space=pl.ANY)],
        compiler_params=LIMIT,
        name="behind",
    )(one, order)


def local(volume, kernel):
    filters, channels = kernel.shape[3], kernel.shape[4]
    shard, _, height, across = volume.shape
    half = channels // 2
    cells = shard * height
    own = volume.reshape(cells, across)
    other = lax.ppermute(own, "chan", [(i, (i + X) % (2 * X)) for i in range(2 * X)])
    s1, s3, s2 = [from_x(own, step) for step in (1, 3, 2)]
    weights = jax.ShapeDtypeStruct((9 * filters, 9 * half), BF16)
    last_weights = jax.ShapeDtypeStruct((9 * filters, 3 * half), BF16)
    near_taps, far_taps, last_taps = pl.pallas_call(
        taps_kernel,
        out_shape=(weights, weights, last_weights),
        compiler_params=LIMIT,
        cost_estimate=pl.CostEstimate(flops=0, bytes_accessed=4_000_000, transcendentals=0),
        name="taps",
    )(kernel)

    part = jax.ShapeDtypeStruct((cells // 2, across), F32)
    low, high = pl.pallas_call(
        divide_kernel,
        out_shape=(part, part),
        in_specs=[pl.BlockSpec(memory_space=pltpu.VMEM), pl.BlockSpec(memory_space=pl.ANY)],
        compiler_params=LIMIT,
        name="divide",
    )(other, last_taps)
    t3a, t1b = from_x(low, 3), from_x(high, 1)

    def work(planes, part):
        return pl.CostEstimate(
            flops=int(2 * 3 * planes * filters * 9 * half * part * height * across),
            bytes_accessed=3_000_000,
            transcendentals=0,
        )

    total = jax.ShapeDtypeStruct((3 * filters, (height + 2) * across), F32)
    packed = pltpu.VMEM((6 * half, height * across), BF16)
    before = pl.pallas_call(
        near_kernel,
        out_shape=total,
        scratch_shapes=[packed],
        compiler_params=LIMIT,
        cost_estimate=work(3, 1),
        name="near",
    )(own, s1, s2, s3, near_taps)
    t2a, t2b = from_x(behind(t3a, before), 3), from_x(behind(t1b, before), 1)
    t3b, t1a = from_x(behind(high, t1b), 3), from_x(behind(low, t3a), 1)
    before = pl.pallas_call(
        far_kernel,
        out_shape=total,
        scratch_shapes=[packed],
        compiler_params=LIMIT,
        cost_estimate=work(3, 1),
        name="far",
    )(other, t1b, t2a, t2b, t3a, far_taps, before)

    def last(name, *taps):
        part = jax.ShapeDtypeStruct((filters * height, across), F32)
        return pl.pallas_call(
            functools.partial(last_kernel, taps),
            out_shape=[part] * len(taps),
            scratch_shapes=[
                pltpu.VMEM((3 * half, height * across), BF16),
                pltpu.VMEM((len(taps) * filters, total.shape[1]), F32),
            ],
            compiler_params=LIMIT,
            cost_estimate=work(len(taps), 0.25),
            name=name,
        )(t1a, t3b, last_taps, before)

    off, on, mid = last("last", 0, 1, 2)
    planes = lax.axis_size("depth")
    between = [(i, i + 1) for i in range(1, planes - 1, 2)]
    within = [(i, i + 1) for i in range(0, planes, 2)]
    pairs = []
    for c in range(2 * X):
        pairs += [(c * planes + i, c * planes + j) for k, l in between for i, j in ((k, l), (l, k))]
        pairs += [(c * planes + d, (c ^ 1) * planes + d) for d in (0, planes - 1)]
    off = lax.ppermute(off, ("chan", "depth"), pairs)
    on = lax.ppermute(on, "depth", within + [(j, i) for i, j in within])
    return (mid + off + on).reshape(filters, 1, height, across)


def solution(mesh):
    return jax.shard_map(
        local,
        mesh=mesh,
        in_specs=(P("chan", "depth", None, None), P(None, None, None, "chan", None)),
        out_specs=P("chan", "depth", None, None),
        check_vma=False,
    )
```

```python
import functools

import jax
import jax.numpy as jnp
from jax import lax
from jax.experimental import pallas as pl
from jax.experimental.pallas import tpu as pltpu
from jax.sharding import PartitionSpec as P

X = 4
ROWS = 2
F32, BF16 = jnp.float32, jnp.bfloat16


def split(values):
    high = values.astype(BF16)
    return high, (values - high.astype(F32)).astype(BF16)


def taps_kernel(kernel_ref, near_ref, far_ref, last_ref):
    me = lax.axis_index("chan")
    core = lax.rem(lax.axis_index("depth"), 2)
    z, x = me // X, lax.rem(me, X)
    filters = kernel_ref.shape[3]
    half = kernel_ref.shape[4] // 2
    shard = half // X
    turn = lax.rem((X - x) * shard, half)
    slot = lax.broadcasted_iota(jnp.int32, (filters, half), 1) // shard
    for out_ref, row in ((near_ref, z), (far_ref, 1 - z)):
        columns = pl.ds(pl.multiple_of(row * half, half), half)
        for a, plane in enumerate((2 - 2 * core, 2 * core, 1)):
            for b in range(3):
                rows = pl.ds((a * 3 + b) * filters, filters)
                blocks = []
                for e in range(3):
                    values = pltpu.roll(kernel_ref[plane, b, e, :, columns], turn, 1)
                    high, low = split(values)
                    out_ref[rows, pl.ds(e * half, half)] = high
                    out_ref[rows, pl.ds((3 + e) * half, half)] = high
                    out_ref[rows, pl.ds((6 + e) * half, half)] = low
                    blocks.append((high.astype(F32), low.astype(F32)))
                if out_ref is far_ref:
                    blocks = [h for h, _ in blocks] * 2 + [l for _, l in blocks]
                    for tile in range(last_ref.shape[1] // half):
                        result = jnp.zeros((filters, half), F32)
                        for k, values in enumerate(blocks[tile * X : tile * X + X]):
                            placed = pltpu.roll(values, (k + X - 2) % X * shard, 1)
                            result = jnp.where(slot == k, placed, result)
                        last_ref[rows, pl.ds(tile * half, half)] = result.astype(BF16)


def pack(ref, cells, h, height, row_sets):
    channels, across = ref.shape[0] // height, ref.shape[1]
    lane = lax.broadcasted_iota(jnp.int32, (channels, across), 1)
    middle = ref[pl.ds(h, channels, stride=height), :]
    left = jnp.where(lane == 0, 0.0, pltpu.roll(middle, 1, 1))
    right = jnp.where(lane == across - 1, 0.0, pltpu.roll(middle, across - 1, 1))
    for values, rows in zip((left, middle, right), row_sets):
        high, low = split(values)
        for row, part in zip(rows, (high, low, high)):
            cells[pl.ds(row, channels), pl.ds(h * across, across)] = part


def accumulate(shards, taps_ref, cells, total):
    across = shards[0][0].shape[1]
    height = cells.shape[1] // across
    half = cells.shape[0] // 6
    channels = half // X
    for k, refs in enumerate(shards):
        if not refs:
            for e in range(6):
                rows = pl.ds(e * half + k * channels, channels)
                cells[rows, :] = jnp.zeros((channels, cells.shape[1]), BF16)
    for start in range(0, height, ROWS):
        for h in range(start, start + ROWS):
            for k, refs in enumerate(shards):
                for j, ref in enumerate(refs):
                    row = k * channels + j * channels // len(refs)
                    pack(ref, cells, h, height, [(e * half + row, (3 + e) * half + row) for e in range(3)])
        wide = pl.ds(start * across, ROWS * across)
        products = jnp.dot(
            taps_ref[:, : 6 * half], cells[:, wide], preferred_element_type=F32
        ) + jnp.dot(
            taps_ref[:, 6 * half :], cells[: 3 * half, wide], preferred_element_type=F32
        )
        scatter(products, total, total.shape[0] // 3, start, across)


def scatter(products, total, filters, start, across):
    for a in range(total.shape[0] // filters):
        for b in range(3):
            row = (a * 3 + b) * filters
            place = pl.ds((start + 2 - b) * across, ROWS * across)
            total[pl.ds(a * filters, filters), place] += products[row : row + filters]


def near_kernel(s0, s1, s2, s3, taps_ref, total, cells):
    total[...] = jnp.zeros_like(total)
    accumulate(((s0,), (s1,), (s2,), (s3,)), taps_ref, cells, total)


def far_kernel(s0, s1a, s1b, s3a, s3b, taps_ref, near_ref, total, cells):
    total[...] = near_ref[...]
    accumulate(((s0,), (s1a, s1b), (), (s3a, s3b)), taps_ref, cells, total)


def last_kernel(planes, s2a, s2b, taps_ref, before_ref, *rest):
    *out_refs, cells, total = rest
    across = s2a.shape[1]
    height = cells.shape[1] // across
    part = s2a.shape[0] // height
    channels = 2 * part
    filters = before_ref.shape[0] // 3
    first = planes[0] * filters
    total[...] = before_ref[pl.ds(first, total.shape[0]), :]
    unused = cells.shape[0] - 9 * channels
    cells[pl.ds(9 * channels, unused), :] = jnp.zeros((unused, cells.shape[1]), BF16)
    for start in range(0, height, ROWS):
        for h in range(start, start + ROWS):
            for j, ref in enumerate((s2a, s2b)):
                rows = [[(3 * t + e) * channels + j * part for t in range(3)] for e in range(3)]
                pack(ref, cells, h, height, rows)
        products = jnp.dot(
            taps_ref[pl.ds(3 * first, 3 * total.shape[0]), :],
            cells[:, pl.ds(start * across, ROWS * across)],
            preferred_element_type=F32,
        )
        scatter(products, total, filters, start, across)
    depth = lax.axis_index("depth")
    edge = (depth == 0) | (depth == lax.axis_size("depth") - 1)
    for a, out_ref in enumerate(out_refs):
        for h in range(height):
            values = total[pl.ds(a * filters, filters), pl.ds((h + 1) * across, across)]
            if planes[a] == 0:
                values = jnp.where(edge, 0.0, values)
            out_ref[pl.ds(h, filters, stride=height), :] = values


def from_x(block, step):
    pairs = [(g * X + i, g * X + (i - step) % X) for g in range(2) for i in range(X)]
    return lax.ppermute(block, "chan", pairs)


def divide_kernel(whole_ref, order_ref, low_ref, high_ref):
    low_ref[...] = whole_ref[: low_ref.shape[0]]
    high_ref[...] = whole_ref[low_ref.shape[0] :]


def local(volume, kernel):
    filters, channels = kernel.shape[3], kernel.shape[4]
    shard, _, height, across = volume.shape
    half = channels // 2
    cells = shard * height
    limit = pltpu.CompilerParams(vmem_limit_bytes=24 * 1024 * 1024)
    own = volume.reshape(cells, across)
    other = lax.ppermute(own, "chan", [(i, (i + X) % (2 * X)) for i in range(2 * X)])
    s1, s3, s2 = [from_x(own, step) for step in (1, 3, 2)]
    weights = jax.ShapeDtypeStruct((9 * filters, 9 * half), BF16)
    last_weights = jax.ShapeDtypeStruct((9 * filters, 3 * half), BF16)
    near_taps, far_taps, last_taps = pl.pallas_call(
        taps_kernel,
        out_shape=(weights, weights, last_weights),
        compiler_params=limit,
        cost_estimate=pl.CostEstimate(flops=0, bytes_accessed=4_000_000, transcendentals=0),
        name="taps",
    )(kernel)

    part = jax.ShapeDtypeStruct((cells // 2, across), F32)
    low, high = pl.pallas_call(
        divide_kernel,
        out_shape=(part, part),
        in_specs=[pl.BlockSpec(memory_space=pltpu.VMEM), pl.BlockSpec(memory_space=pl.ANY)],
        compiler_params=limit,
        name="divide",
    )(other, last_taps)
    t3a, t1b = from_x(low, 3), from_x(high, 1)
    t3b, t1a = from_x(high, 3), from_x(low, 1)
    t2a, t2b = from_x(t3a, 3), from_x(t1b, 1)

    def work(planes, part):
        return pl.CostEstimate(
            flops=int(2 * 3 * planes * filters * 9 * half * part * height * across),
            bytes_accessed=3_000_000,
            transcendentals=0,
        )

    total = jax.ShapeDtypeStruct((3 * filters, (height + 2) * across), F32)
    packed = pltpu.VMEM((6 * half, height * across), BF16)
    before = pl.pallas_call(
        near_kernel,
        out_shape=total,
        scratch_shapes=[packed],
        compiler_params=limit,
        cost_estimate=work(3, 1),
        name="near",
    )(own, s1, s2, s3, near_taps)
    before = pl.pallas_call(
        far_kernel,
        out_shape=total,
        scratch_shapes=[packed],
        compiler_params=limit,
        cost_estimate=work(3, 4),
        name="far",
    )(other, t1a, t1b, t3a, t3b, far_taps, before)

    def last(name, *taps):
        part = jax.ShapeDtypeStruct((filters * height, across), F32)
        return pl.pallas_call(
            functools.partial(last_kernel, taps),
            out_shape=[part] * len(taps),
            scratch_shapes=[
                pltpu.VMEM((3 * half, height * across), BF16),
                pltpu.VMEM((len(taps) * filters, total.shape[1]), F32),
            ],
            compiler_params=limit,
            cost_estimate=work(len(taps), 0.25),
            name=name,
        )(t2a, t2b, last_taps, before)

    (off,) = last("off", 0)
    on, mid = last("rest", 1, 2)
    planes = lax.axis_size("depth")
    between = [(i, i + 1) for i in range(1, planes - 1, 2)]
    within = [(i, i + 1) for i in range(0, planes, 2)]
    pairs = []
    for c in range(2 * X):
        pairs += [(c * planes + i, c * planes + j) for k, l in between for i, j in ((k, l), (l, k))]
        pairs += [(c * planes + d, (c ^ 1) * planes + d) for d in (0, planes - 1)]
    off = lax.ppermute(off, ("chan", "depth"), pairs)
    on = lax.ppermute(on, "depth", within + [(j, i) for i, j in within])
    return (mid + off + on).reshape(filters, 1, height, across)


def solution(mesh):
    return jax.shard_map(
        local,
        mesh=mesh,
        in_specs=(P("chan", "depth", None, None), P(None, None, None, "chan", None)),
        out_specs=P("chan", "depth", None, None),
        check_vma=False,
    )
```

```python
import functools

import jax
import jax.numpy as jnp
from jax import lax
from jax.experimental import pallas as pl
from jax.experimental.pallas import tpu as pltpu
from jax.sharding import PartitionSpec as P

X = 4
ROWS = 4
F32, BF16 = jnp.float32, jnp.bfloat16


def split(values):
    high = values.astype(BF16)
    return high, (values - high.astype(F32)).astype(BF16)


def taps_kernel(kernel_ref, near_ref, far_ref, last_ref):
    me = lax.axis_index("chan")
    core = lax.rem(lax.axis_index("depth"), 2)
    z, x = me // X, lax.rem(me, X)
    filters = kernel_ref.shape[3]
    half = kernel_ref.shape[4] // 2
    shard = half // X
    turn = lax.rem((X - x) * shard, half)
    slot = lax.broadcasted_iota(jnp.int32, (filters, half), 1) // shard
    for out_ref, row in ((near_ref, z), (far_ref, 1 - z)):
        columns = pl.ds(pl.multiple_of(row * half, half), half)
        for a, plane in enumerate((2 - 2 * core, 2 * core, 1)):
            for b in range(3):
                rows = pl.ds((a * 3 + b) * filters, filters)
                blocks = []
                for e in range(3):
                    values = pltpu.roll(kernel_ref[plane, b, e, :, columns], turn, 1)
                    high, low = split(values)
                    out_ref[rows, pl.ds(e * half, half)] = high
                    out_ref[rows, pl.ds((3 + e) * half, half)] = high
                    out_ref[rows, pl.ds((6 + e) * half, half)] = low
                    blocks.append((high.astype(F32), low.astype(F32)))
                if out_ref is far_ref:
                    blocks = [h for h, _ in blocks] * 2 + [l for _, l in blocks]
                    for tile in range(last_ref.shape[1] // half):
                        result = jnp.zeros((filters, half), F32)
                        for k, values in enumerate(blocks[tile * X : tile * X + X]):
                            placed = pltpu.roll(values, (k + X - 2) % X * shard, 1)
                            result = jnp.where(slot == k, placed, result)
                        last_ref[rows, pl.ds(tile * half, half)] = result.astype(BF16)


def pack(ref, cells, h, height, row_sets):
    channels, across = ref.shape[0] // height, ref.shape[1]
    lane = lax.broadcasted_iota(jnp.int32, (channels, across), 1)
    middle = ref[pl.ds(h, channels, stride=height), :]
    left = jnp.where(lane == 0, 0.0, pltpu.roll(middle, 1, 1))
    right = jnp.where(lane == across - 1, 0.0, pltpu.roll(middle, across - 1, 1))
    for values, rows in zip((left, middle, right), row_sets):
        high, low = split(values)
        for row, part in zip(rows, (high, low, high)):
            cells[pl.ds(row, channels), pl.ds(h * across, across)] = part


def accumulate(shards, taps_ref, cells, total):
    across = shards[0][0].shape[1]
    height = cells.shape[1] // across
    half = cells.shape[0] // 6
    channels = half // X
    for k, refs in enumerate(shards):
        if not refs:
            for e in range(6):
                rows = pl.ds(e * half + k * channels, channels)
                cells[rows, :] = jnp.zeros((channels, cells.shape[1]), BF16)
    for start in range(0, height, ROWS):
        for h in range(start, start + ROWS):
            for k, refs in enumerate(shards):
                for j, ref in enumerate(refs):
                    row = k * channels + j * channels // len(refs)
                    pack(ref, cells, h, height, [(e * half + row, (3 + e) * half + row) for e in range(3)])
        wide = pl.ds(start * across, ROWS * across)
        products = jnp.dot(
            taps_ref[:, : 6 * half], cells[:, wide], preferred_element_type=F32
        ) + jnp.dot(
            taps_ref[:, 6 * half :], cells[: 3 * half, wide], preferred_element_type=F32
        )
        scatter(products, total, total.shape[0] // 3, start, across)


def scatter(products, total, filters, start, across):
    for a in range(total.shape[0] // filters):
        for b in range(3):
            row = (a * 3 + b) * filters
            place = pl.ds((start + 2 - b) * across, ROWS * across)
            total[pl.ds(a * filters, filters), place] += products[row : row + filters]


def near_kernel(s0, s1, s2, s3, taps_ref, total, cells):
    total[...] = jnp.zeros_like(total)
    accumulate(((s0,), (s1,), (s2,), (s3,)), taps_ref, cells, total)


def far_kernel(s0, s1a, s1b, s3a, s3b, taps_ref, near_ref, total, cells):
    total[...] = near_ref[...]
    accumulate(((s0,), (s1a, s1b), (), (s3a, s3b)), taps_ref, cells, total)


def last_kernel(planes, s2a, s2b, taps_ref, before_ref, *rest):
    *out_refs, cells, total = rest
    across = s2a.shape[1]
    height = cells.shape[1] // across
    part = s2a.shape[0] // height
    channels = 2 * part
    filters = before_ref.shape[0] // 3
    first = planes[0] * filters
    total[...] = before_ref[pl.ds(first, total.shape[0]), :]
    unused = cells.shape[0] - 9 * channels
    cells[pl.ds(9 * channels, unused), :] = jnp.zeros((unused, cells.shape[1]), BF16)
    for start in range(0, height, ROWS):
        for h in range(start, start + ROWS):
            for j, ref in enumerate((s2a, s2b)):
                rows = [[(3 * t + e) * channels + j * part for t in range(3)] for e in range(3)]
                pack(ref, cells, h, height, rows)
        products = jnp.dot(
            taps_ref[pl.ds(3 * first, 3 * total.shape[0]), :],
            cells[:, pl.ds(start * across, ROWS * across)],
            preferred_element_type=F32,
        )
        scatter(products, total, filters, start, across)
    depth = lax.axis_index("depth")
    edge = (depth == 0) | (depth == lax.axis_size("depth") - 1)
    for a, out_ref in enumerate(out_refs):
        for h in range(height):
            values = total[pl.ds(a * filters, filters), pl.ds((h + 1) * across, across)]
            if planes[a] == 0:
                values = jnp.where(edge, 0.0, values)
            out_ref[pl.ds(h, filters, stride=height), :] = values


def from_x(block, step):
    pairs = [(g * X + i, g * X + (i - step) % X) for g in range(2) for i in range(X)]
    return lax.ppermute(block, "chan", pairs)


def divide_kernel(whole_ref, order_ref, low_ref, high_ref):
    low_ref[...] = whole_ref[: low_ref.shape[0]]
    high_ref[...] = whole_ref[low_ref.shape[0] :]


def local(volume, kernel):
    filters, channels = kernel.shape[3], kernel.shape[4]
    shard, _, height, across = volume.shape
    half = channels // 2
    cells = shard * height
    limit = pltpu.CompilerParams(vmem_limit_bytes=24 * 1024 * 1024)
    own = volume.reshape(cells, across)
    other = lax.ppermute(own, "chan", [(i, (i + X) % (2 * X)) for i in range(2 * X)])
    s1, s3, s2 = [from_x(own, step) for step in (1, 3, 2)]
    weights = jax.ShapeDtypeStruct((9 * filters, 9 * half), BF16)
    last_weights = jax.ShapeDtypeStruct((9 * filters, 3 * half), BF16)
    near_taps, far_taps, last_taps = pl.pallas_call(
        taps_kernel,
        out_shape=(weights, weights, last_weights),
        compiler_params=limit,
        cost_estimate=pl.CostEstimate(flops=0, bytes_accessed=4_000_000, transcendentals=0),
        name="taps",
    )(kernel)

    part = jax.ShapeDtypeStruct((cells // 2, across), F32)
    low, high = pl.pallas_call(
        divide_kernel,
        out_shape=(part, part),
        in_specs=[pl.BlockSpec(memory_space=pltpu.VMEM), pl.BlockSpec(memory_space=pl.ANY)],
        compiler_params=limit,
        name="divide",
    )(other, last_taps)
    t3a, t1b = from_x(low, 3), from_x(high, 1)
    t3b, t1a = from_x(high, 3), from_x(low, 1)
    t2a, t2b = from_x(t3a, 3), from_x(t1b, 1)

    def work(planes, part):
        return pl.CostEstimate(
            flops=int(2 * 3 * planes * filters * 9 * half * part * height * across),
            bytes_accessed=3_000_000,
            transcendentals=0,
        )

    total = jax.ShapeDtypeStruct((3 * filters, (height + 2) * across), F32)
    packed = pltpu.VMEM((6 * half, height * across), BF16)
    before = pl.pallas_call(
        near_kernel,
        out_shape=total,
        scratch_shapes=[packed],
        compiler_params=limit,
        cost_estimate=work(3, 1),
        name="near",
    )(own, s1, s2, s3, near_taps)
    before = pl.pallas_call(
        far_kernel,
        out_shape=total,
        scratch_shapes=[packed],
        compiler_params=limit,
        cost_estimate=work(3, 4),
        name="far",
    )(other, t1a, t1b, t3a, t3b, far_taps, before)

    def last(name, *taps):
        part = jax.ShapeDtypeStruct((filters * height, across), F32)
        return pl.pallas_call(
            functools.partial(last_kernel, taps),
            out_shape=[part] * len(taps),
            scratch_shapes=[
                pltpu.VMEM((3 * half, height * across), BF16),
                pltpu.VMEM((len(taps) * filters, total.shape[1]), F32),
            ],
            compiler_params=limit,
            cost_estimate=work(len(taps), 0.25),
            name=name,
        )(t2a, t2b, last_taps, before)

    (off,) = last("off", 0)
    on, mid = last("rest", 1, 2)
    planes = lax.axis_size("depth")
    between = [(i, i + 1) for i in range(1, planes - 1, 2)]
    within = [(i, i + 1) for i in range(0, planes, 2)]
    pairs = []
    for c in range(2 * X):
        pairs += [(c * planes + i, c * planes + j) for k, l in between for i, j in ((k, l), (l, k))]
        pairs += [(c * planes + d, (c ^ 1) * planes + d) for d in (0, planes - 1)]
    off = lax.ppermute(off, ("chan", "depth"), pairs)
    on = lax.ppermute(on, "depth", within + [(j, i) for i, j in within])
    return (mid + off + on).reshape(filters, 1, height, across)


def solution(mesh):
    return jax.shard_map(
        local,
        mesh=mesh,
        in_specs=(P("chan", "depth", None, None), P(None, None, None, "chan", None)),
        out_specs=P("chan", "depth", None, None),
        check_vma=False,
    )
```
